256 devices in a mesh: member: 4 (over y_hi, core), point: 64 (over x, y_lo, z).
Axes of the slice: x: 4, y: 4 (y_hi: 2, y_lo: 2; y = y_hi * 2 + y_lo), z: 8, core: 2. Of those that a mesh axis runs over, the one named last changes fastest.
Arguments:
- final_hidden_states: bfloat16 [16, 49152, 1024], P('member', 'point'), may hold values from -16 to 16
- readout_weights_table: bfloat16 [1024, 100], replicated, may hold values from -0.1875 to 0.1875
- readout_shift: float32 [100], replicated, may hold values from -3 to 3
- observed_truth: float32 [49152, 100], P('point'), may hold values from -6 to 6
- area: float32 [49152], P('point'), may hold values from 0.25 to 4
- quantity_coefficient: float32 [100], replicated, may hold values from 0.25 to 4
Outputs:
- objective_value: float32 [], replicated
- hidden_state_slope: bfloat16 [16, 49152, 1024], P('member', 'point')
- normalised_projection_derivative: float32 [1024, 100], P(('member', 'point'))
- grad_bias: float32 [100], replicated
The draws below stay inside these ranges and needn't reach their ends.
All inputs are finite; a program needn't handle non-finite values.
Results may differ from the reference program's by a relative error of at most 0.0049.
Values may be sent and summed in bfloat16 or wider, within the bound.
No kernel may reach another device: no remote copies, remote signals or barrier semaphores. Data moves between devices by JAX's collectives and lax.ppermute only.
A program may use at most 128 MiB of HBM per device.

```python
import math
import jax
import jax.numpy as jnp
from jax import lax

HIDDEN_WIDTHS_N = 1024
TARGET_FIELDS_N = 100
M = 16
CELL_COUNT = 49152


def strengthened(values, key, source, target, blocks, factor):
    def block_of(dim):
        return (jnp.arange(values.shape[dim]) // (values.shape[dim] // blocks)).reshape((-1,) + (1,) * (values.ndim - 1 - dim))

    first = jax.random.permutation(key, blocks)[block_of(target)]
    far = (block_of(target) + blocks // 2) % blocks
    return jnp.where((block_of(source) == first) | (block_of(source) == far), factor * values, values)


def level_of(rng, dims, pieces, low, largest):
    loudness = 1.0
    for dim, shards_of in pieces:
        heights = jax.random.uniform(jax.random.fold_in(jax.random.fold_in(rng, 6), dim), (shards_of,), jnp.float32, low / len(pieces), largest / len(pieces))
        loudness = loudness * jnp.repeat(jnp.exp(heights), dims[dim] // shards_of).reshape((-1,) + (1,) * (len(dims) - 1 - dim))
    return loudness


def gaussian(stream_key, shape, scale, most, cuts=(), kind=jnp.bfloat16):
    drawn = scale * jax.random.normal(stream_key, shape, jnp.float32)
    if cuts:
        drawn = drawn * level_of(stream_key, shape, cuts, -0.22, 0.18)
    return jnp.clip(drawn, -most, most).astype(kind)


def gaussian_with(rng, extent, deviation, most, split, heavy, dtype=jnp.bfloat16):
    result = deviation * jax.random.normal(rng, extent, jnp.float32)
    if split:
        result = result * level_of(rng, extent, split, -0.22, 0.18)
    return jnp.clip(strengthened(result, jax.random.fold_in(rng, 3), *heavy), -most, most).astype(dtype)


def setup_inputs(seed: int = 0) -> dict:
    key_list = jax.random.split(jax.random.key(seed), 7)
    return {
        "final_hidden_states": gaussian_with(key_list[0], (M, CELL_COUNT, HIDDEN_WIDTHS_N), 1.0, 16.0, ((0, 4), (1, 64)), (1, 2, 64, 4.0)),
        "readout_weights_table": gaussian(key_list[1], (HIDDEN_WIDTHS_N, TARGET_FIELDS_N), HIDDEN_WIDTHS_N ** -0.5, 0.1875),
        "readout_shift": gaussian(key_list[2], (TARGET_FIELDS_N,), 0.5, 3.0, (), jnp.float32),
        "observed_truth": gaussian(key_list[3], (CELL_COUNT, TARGET_FIELDS_N), 1.0, 6.0, ((0, 64),), jnp.float32),
        "area": jnp.clip(jnp.exp(math.log(4.0) - 2.7725887 * jax.random.uniform(key_list[4], (CELL_COUNT,), jnp.float32) ** level_of(key_list[4], (CELL_COUNT,), ((0, 64),), -0.2, 0.2)), 0.25, 4.0),
        "quantity_coefficient": jnp.clip(jnp.exp(jax.random.uniform(key_list[5], (TARGET_FIELDS_N,), jnp.float32, math.log(0.25), math.log(4.0))), 0.25, 4.0),
    }


blurring_operator = 0.05
blend_factor_crps = 0.95

def couple_totals(collected_replicas):

    def append_replica(index, carry):
        polarity_slopes_table, blurring_lengths = carry
        other = lax.dynamic_index_in_dim(collected_replicas, index, 0, keepdims=True)
        draw_discrepancy = collected_replicas - other
        blurring_half_width = jnp.sqrt(draw_discrepancy * draw_discrepancy + blurring_operator * blurring_operator)
        return (polarity_slopes_table + draw_discrepancy / blurring_half_width, blurring_lengths + blurring_half_width)
    empty_start = jnp.zeros(collected_replicas.shape, jnp.float32)
    return lax.fori_loop(0, collected_replicas.shape[0], append_replica, (empty_start, empty_start))

def reference(final_hidden_states, readout_weights_table, readout_shift, observed_truth, area, quantity_coefficient):
    drawn_estimates = final_hidden_states.shape[0]
    affine_estimate_array = final_hidden_states.reshape(-1, HIDDEN_WIDTHS_N)
    estimate_layout = jnp.dot(affine_estimate_array, readout_weights_table, preferred_element_type=jnp.float32).reshape(drawn_estimates, CELL_COUNT, TARGET_FIELDS_N) + readout_shift
    polarity_slopes_table, blurring_lengths = couple_totals(estimate_layout)
    draw_discrepancy = estimate_layout - observed_truth[None]
    blurring_half_width = jnp.sqrt(draw_discrepancy * draw_discrepancy + blurring_operator * blurring_operator)
    corrected_blend_factor = (1.0 - blend_factor_crps) / drawn_estimates
    accuracy_term = lax.optimization_barrier(jnp.mean(blurring_half_width, axis=0))
    dispersion_term = lax.optimization_barrier(jnp.sum(blurring_lengths, axis=0)) - drawn_estimates * blurring_operator
    continuous_rank_loss = accuracy_term - (1.0 - corrected_blend_factor) / (2.0 * drawn_estimates * (drawn_estimates - 1)) * dispersion_term
    cell_factor_table = area[:, None] * quantity_coefficient[None, :]
    objective_value = jnp.sum(cell_factor_table * continuous_rank_loss) / (CELL_COUNT * TARGET_FIELDS_N)
    estimate_response = (cell_factor_table[None] * (draw_discrepancy / blurring_half_width - (1.0 - corrected_blend_factor) / (drawn_estimates - 1) * polarity_slopes_table)).astype(jnp.bfloat16)
    affine_response_array = estimate_response.reshape(-1, TARGET_FIELDS_N)
    hidden_state_slope = jnp.dot(affine_response_array, readout_weights_table.T, preferred_element_type=jnp.float32).astype(jnp.bfloat16).reshape(drawn_estimates, CELL_COUNT, HIDDEN_WIDTHS_N)
    scaling_factor = 1.0 / jnp.sqrt(jnp.float32(drawn_estimates * CELL_COUNT))
    normalised_projection_derivative = lax.dot_general(affine_estimate_array, affine_response_array, (((0,), (0,)), ((), ())), preferred_element_type=jnp.float32) * scaling_factor
    grad_bias = lax.optimization_barrier(jnp.sum(affine_response_array.astype(jnp.float32), axis=0)) * scaling_factor
    return (objective_value, hidden_state_slope, normalised_projection_derivative, grad_bias)
```

```python
import functools

import jax
import jax.numpy as jnp
from jax import lax
from jax.experimental import pallas as pl
from jax.experimental.pallas import tpu as pltpu
from jax.sharding import PartitionSpec as P

F32 = jnp.float32
BF16 = jnp.bfloat16
LANES = 128
TILES = (6,)
SMOOTH = 0.05 * 0.05
ALPHA = 0.95
VMEM_LIMIT = 48 * 1024 * 1024


def params():
    return pltpu.CompilerParams(vmem_limit_bytes=VMEM_LIMIT)


def round_up(n, k):
    return -(-n // k) * k


def forecast_kernel(x_ref, w_ref, own_ref, sent_ref, wpad, wt):
    members, _, width = x_ref.shape
    rows = own_ref.shape[1]
    fields = w_ref.shape[1]

    @pl.when(pl.program_id(0) == 0)
    def _():
        wpad[...] = jnp.zeros_like(wpad)
        wpad[:, :fields] = w_ref[...]
        wt[...] = wpad[...].T

    x = x_ref[...].reshape(members * LANES, width)
    f = lax.dot_general(
        wt[...], x, (((1,), (1,)), ((), ())), preferred_element_type=F32
    )[:rows]
    own_ref[0] = f
    groups = [
        f[8 * g : 8 * g + 8, m * LANES : (m + 1) * LANES]
        for g in range(rows // 8)
        for m in range(members)
    ]
    sent_ref[0] = jnp.concatenate(groups, axis=0).astype(BF16)


def column(row, rows):
    return jnp.broadcast_to(row, (LANES, LANES)).T[:rows]


def pad_row(ref, scratch, fields):
    scratch[...] = jnp.zeros_like(scratch)
    scratch[:, :fields] = ref[...]
    return scratch[...]


def slope_and_length(d):
    t = d * d + SMOOTH
    r = lax.rsqrt(t)
    return d * r, t * r


def near_kernel(own_ref, sib_ref, truth_ref, area_ref, shift_ref, coef_ref, acc_ref, loss_ref, tpad, rpad, shifts, coefs, *, members, total):
    rows = own_ref.shape[1]
    fields = truth_ref.shape[1]
    c1 = (1.0 - (1.0 - ALPHA) / total) / (total - 1)
    c2 = (1.0 - (1.0 - ALPHA) / total) / (2.0 * total * (total - 1))

    @pl.when(pl.program_id(0) == 0)
    def _():
        shifts[...] = column(pad_row(shift_ref, rpad, fields), rows)
        coefs[...] = column(pad_row(coef_ref, rpad, fields), rows)
        tpad[...] = jnp.zeros_like(tpad)
        loss_ref[...] = jnp.zeros_like(loss_ref)

    tpad[:, :fields] = truth_ref[...]
    truth = tpad[...].T[:rows] - shifts[...]
    loss = jnp.zeros((8, LANES), F32)
    for g in range(rows // 8):
        span = slice(8 * g, 8 * g + 8)
        own = [own_ref[0, span, m * LANES : (m + 1) * LANES] for m in range(members)]
        sib = sib_ref[0, 8 * members * g : 8 * members * (g + 1), :].astype(F32)
        skill = jnp.zeros((8, LANES), F32)
        spread = jnp.zeros((8, LANES), F32)
        inner = jnp.zeros((8, LANES), F32)
        slopes = [jnp.zeros((8, LANES), F32) for _ in range(members)]
        for m in range(members):
            for n in range(m + 1, members):
                a, b = slope_and_length(own[m] - own[n])
                slopes[m] = slopes[m] + a
                slopes[n] = slopes[n] - a
                inner = inner + b
            for n in range(members):
                a, b = slope_and_length(own[m] - sib[8 * n : 8 * n + 8])
                slopes[m] = slopes[m] + a
                spread = spread + b
        for m in range(members):
            a, b = slope_and_length(own[m] - truth[span])
            skill = skill + b
            acc_ref[0, span, m * LANES : (m + 1) * LANES] = a - c1 * slopes[m]
        loss = loss + coefs[span] * (skill * (1.0 / total) - c2 * (spread + 2.0 * inner))
    loss_ref[...] += loss * area_ref[...]


def far_kernel(own_ref, far_ref, fwd_ref, acc_ref, area_ref, coef_ref, x_ref, grad_ref, dw_ref, bias_ref, loss_ref, rpad, coefs, grads, *, members, total):
    rows = own_ref.shape[1]
    fields = coef_ref.shape[1]
    width = x_ref.shape[2]
    c1 = (1.0 - (1.0 - ALPHA) / total) / (total - 1)
    c2 = (1.0 - (1.0 - ALPHA) / total) / (2.0 * total * (total - 1))

    @pl.when(pl.program_id(0) == 0)
    def _():
        coefs[...] = column(pad_row(coef_ref, rpad, fields), rows)
        loss_ref[...] = jnp.zeros_like(loss_ref)
        dw_ref[...] = jnp.zeros_like(dw_ref)
        bias_ref[...] = jnp.zeros_like(bias_ref)
        grads[...] = jnp.zeros_like(grads)

    area = jnp.broadcast_to(area_ref[...], (8, LANES))
    loss = jnp.zeros((8, LANES), F32)
    for g in range(rows // 8):
        span = slice(8 * g, 8 * g + 8)
        part = slice(8 * members * g, 8 * members * (g + 1))
        own = [own_ref[0, span, m * LANES : (m + 1) * LANES] for m in range(members)]
        far = far_ref[0, part, :].astype(F32)
        fwd = fwd_ref[0, part, :].astype(F32)
        spread = jnp.zeros((8, LANES), F32)
        scale = coefs[span] * area
        bias = jnp.zeros((8, LANES), F32)
        for m in range(members):
            slopes = jnp.zeros((8, LANES), F32)
            for other in (far, fwd):
                for n in range(members):
                    a, b = slope_and_length(own[m] - other[8 * n : 8 * n + 8])
                    slopes = slopes + a
                    spread = spread + b
            here = slice(m * LANES, (m + 1) * LANES)
            grad = (scale * (acc_ref[0, span, here] - c1 * slopes)).astype(BF16).astype(F32)
            grads[span, here] = grad
            bias = bias + grad
        bias_ref[span, :] += bias
        loss = loss + coefs[span] * spread
    loss_ref[...] -= c2 * loss * area
    grad = grads[...].astype(BF16)
    grad_ref[0] = grad
    dw_ref[...] += jnp.dot(grad, x_ref[...].reshape(members * LANES, width), preferred_element_type=F32)


def pack_kernel(*refs, chunks, fields):
    dws, biases, losses = refs[:chunks], refs[chunks : 2 * chunks], refs[2 * chunks : 4 * chunks]
    out_ref = refs[4 * chunks]
    padded = refs[4 * chunks + 1]
    dw = sum(r[...] for r in dws)
    padded[...] = jnp.zeros_like(padded)
    padded[: biases[0].shape[0], :] = sum(r[...] for r in biases)
    bias = jnp.sum(padded[...].T, axis=0, keepdims=True)
    loss = sum(r[...] for r in losses)
    loss = jnp.sum(jnp.sum(loss, axis=0, keepdims=True), axis=1, keepdims=True)
    high = loss.astype(BF16).astype(F32)
    low = loss - high
    quarter = fields // 4
    lane = lax.broadcasted_iota(jnp.int32, (8, LANES), 1)
    row = lax.broadcasted_iota(jnp.int32, (8, LANES), 0) % 4
    bias = jnp.broadcast_to(bias, (8, LANES))
    extra = jnp.zeros((8, LANES), F32)
    for r in range(4):
        moved = pltpu.roll(bias, fields - quarter * r, 1)
        extra = jnp.where(row == r, moved, extra)
    extra = jnp.where(lane < fields + quarter, extra, 0.0)
    at = lane == fields + quarter
    extra = jnp.where(at & (row == 0), high, extra)
    extra = jnp.where(at & (row == 1), low, extra)
    table = dw.T.reshape(-1, 8, LANES)
    keep = lax.broadcasted_iota(jnp.int32, table.shape, 2) < fields
    table = jnp.where(keep, table, extra[None])
    out_ref[...] = table.reshape(out_ref.shape).astype(BF16)


def slope_kernel(grad_ref, w_ref, out_ref, wpad):
    fields = w_ref.shape[1]

    @pl.when(pl.program_id(0) == 0)
    def _():
        wpad[...] = jnp.zeros_like(wpad)
        wpad[:, :fields] = w_ref[...]

    s = lax.dot_general(
        grad_ref[0], wpad[...], (((0,), (1,)), ((), ())), preferred_element_type=F32
    )
    out_ref[...] = s.astype(BF16).reshape(out_ref.shape)


def finish_kernel(parts_ref, dw_ref, bias_ref, loss_ref, *, fields, scale, count):
    parts = parts_ref[...].astype(F32).reshape(-1, 8, LANES)
    total = jnp.sum(parts, axis=0)
    total = total[:4] + total[4:]
    dw_ref[...] = total[:, :fields] * scale
    quarter = fields // 4
    lane = lax.broadcasted_iota(jnp.int32, (1, LANES), 1)
    bias = jnp.zeros((1, LANES), F32)
    for r in range(4):
        moved = pltpu.roll(total, (quarter * r - fields) % LANES, 1)[r : r + 1]
        bias = jnp.where((lane >= quarter * r) & (lane < quarter * (r + 1)), moved, bias)
    bias_ref[...] = bias[:, :fields] * scale
    at = fields + quarter
    loss_ref[...] = (total[0:1, at : at + 1] + total[1:2, at : at + 1]) * (1.0 / count)


def shards(hidden, weights, shift, truth, area, coef):
    members, points, width = hidden.shape
    fields = weights.shape[1]
    total = members * lax.axis_size("member")
    all_points = points * lax.axis_size("point")
    rows = round_up(fields, 8)
    depth = round_up(fields, 16)
    span = members * LANES
    shift, coef, area = shift[None], coef[None], area[None]
    fixed = lambda shape: pl.BlockSpec(shape, lambda i: (0,) * len(shape))
    tile = lambda shape: pl.BlockSpec((1,) + shape, lambda i: (i, 0, 0))
    shape = jax.ShapeDtypeStruct
    core_swap = [(0, 1), (1, 0), (2, 3), (3, 2)]
    chip_swap = [(0, 2), (1, 3), (2, 0), (3, 1)]

    sent = []
    first = 0
    for n in TILES:
        at = lambda i, first=first: (0, first + i, 0)
        own, out = pl.pallas_call(
            forecast_kernel,
            grid=(n,),
            in_specs=[pl.BlockSpec((members, LANES, width), at), fixed((width, fields))],
            out_specs=[tile((rows, span)), tile((rows * members, LANES))],
            out_shape=[shape((n, rows, span), F32), shape((n, rows * members, LANES), BF16)],
            scratch_shapes=[pltpu.VMEM((width, LANES), BF16), pltpu.VMEM((LANES, width), BF16)],
            compiler_params=params(),
            name="forecast",
        )(hidden, weights)
        far = lax.ppermute(out, "member", chip_swap)
        sib = lax.ppermute(out, "member", core_swap)
        sent.append((n, first, own, far, sib))
        first += n

    near = []
    for n, first, own, far, sib in sent:
        at = lambda i, first=first: (first + i, 0)
        along = lambda i, first=first: (0, first + i)
        acc, loss = pl.pallas_call(
            functools.partial(near_kernel, members=members, total=total),
            grid=(n,),
            in_specs=[
                tile((rows, span)),
                tile((rows * members, LANES)),
                pl.BlockSpec((LANES, fields), at),
                pl.BlockSpec((1, LANES), along),
                fixed((1, fields)),
                fixed((1, fields)),
            ],
            out_specs=[tile((rows, span)), fixed((8, LANES))],
            out_shape=[shape((n, rows, span), F32), shape((8, LANES), F32)],
            scratch_shapes=[
                pltpu.VMEM((LANES, LANES), F32),
                pltpu.VMEM((1, LANES), F32),
                pltpu.VMEM((rows, LANES), F32),
                pltpu.VMEM((rows, LANES), F32),
            ],
            compiler_params=params(),
            name="near",
        )(own, sib, truth, area, shift, coef)
        near.append((acc, loss))

    grads, dws, biases, losses = [], [], [], []
    for (n, first, own, far, _), (acc, loss) in zip(sent, near):
        fwd = lax.ppermute(far, "member", core_swap)
        at = lambda i, first=first: (0, first + i, 0)
        along = lambda i, first=first: (0, first + i)
        grad, dw, bias, far_loss = pl.pallas_call(
            functools.partial(far_kernel, members=members, total=total),
            grid=(n,),
            in_specs=[
                tile((rows, span)),
                tile((rows * members, LANES)),
                tile((rows * members, LANES)),
                tile((rows, span)),
                pl.BlockSpec((1, LANES), along),
                fixed((1, fields)),
                pl.BlockSpec((members, LANES, width), at),
            ],
            out_specs=[tile((LANES, span)), fixed((LANES, width)), fixed((rows, LANES)), fixed((8, LANES))],
            out_shape=[
                shape((n, LANES, span), BF16),
                shape((LANES, width), F32),
                shape((rows, LANES), F32),
                shape((8, LANES), F32),
            ],
            scratch_shapes=[
                pltpu.VMEM((1, LANES), F32),
                pltpu.VMEM((rows, LANES), F32),
                pltpu.VMEM((LANES, span), F32),
            ],
            compiler_params=params(),
            name="far",
        )(own, far, fwd, acc, area, coef, hidden)
        grads.append(grad)
        dws.append(dw)
        biases.append(bias)
        losses += [loss, far_loss]

    packed = pl.pallas_call(
        functools.partial(pack_kernel, chunks=len(TILES), fields=fields),
        out_shape=shape((width, LANES), BF16),
        scratch_shapes=[pltpu.VMEM((LANES, LANES), F32)],
        compiler_params=params(),
        name="pack",
    )(*dws, *biases, *losses)
    parts = lax.all_to_all(packed, ("member", "point"), split_axis=0, concat_axis=0, tiled=True)

    grad = grads[0] if len(grads) == 1 else jnp.concatenate(grads, axis=0)
    slope = pl.pallas_call(
        slope_kernel,
        grid=(points // LANES,),
        in_specs=[tile((LANES, span)), fixed((width, fields))],
        out_specs=pl.BlockSpec((members, LANES, width), lambda i: (0, i, 0)),
        out_shape=shape(hidden.shape, BF16),
        scratch_shapes=[pltpu.VMEM((width, LANES), BF16)],
        compiler_params=params(),
        cost_estimate=pl.CostEstimate(flops=2 * members * points * width * LANES, bytes_accessed=4 * members * points * width, transcendentals=0),
        name="slope",
    )(grad, weights)

    own_rows = width // (lax.axis_size("member") * lax.axis_size("point"))
    dw, bias, loss = pl.pallas_call(
        functools.partial(
            finish_kernel, fields=fields, scale=float((total * all_points) ** -0.5), count=float(all_points * fields)
        ),
        out_shape=[shape((own_rows, fields), F32), shape((1, fields), F32), shape((1, 1), F32)],
        compiler_params=params(),
        name="finish",
    )(parts)
    return loss.reshape(()), slope, dw, bias.reshape(fields)


def solution(mesh):
    placed = (P("member", "point", None), P(), P(), P("point", None), P("point"), P())
    return jax.shard_map(
        shards,
        mesh=mesh,
        in_specs=placed,
        out_specs=(P(), P("member", "point", None), P(("member", "point"), None), P()),
        check_vma=False,
    )
```

```python
import functools

import jax
import jax.numpy as jnp
from jax import lax
from jax.experimental import pallas as pl
from jax.experimental.pallas import tpu as pltpu
from jax.sharding import PartitionSpec as P

F32 = jnp.float32
BF16 = jnp.bfloat16
LANES = 128
TILES = (2, 2, 2)
US = (.01,.01,.01,.01,8,8,.01,8,.01)
SMOOTH = 0.05 * 0.05
ALPHA = 0.95


def params(mib=48):
    return pltpu.CompilerParams(vmem_limit_bytes=mib * 1024 * 1024)


def round_up(n, k):
    return -(-n // k) * k


def forecast_kernel(x_hbm, w_hbm, own_ref, sent_ref, x, w, x_sems, w_sem, *, first):
    tiles, members, _, width = x.shape
    rows = own_ref.shape[1]
    fields = w.shape[0]
    w_copy = pltpu.make_async_copy(w_hbm, w, w_sem)
    w_copy.start()

    def fetch(t):
        points = pl.ds((first + t) * LANES, LANES)
        return pltpu.make_async_copy(x_hbm.at[:, points], x.at[t], x_sems.at[t])

    for t in range(tiles):
        fetch(t).start()
    w_copy.wait()

    def step(t, carry):
        fetch(t).wait()
        f = lax.dot_general(
            x[t].reshape(members * LANES, width),
            w[...],
            (((1,), (1,)), ((), ())),
            preferred_element_type=F32,
        )
        f = jnp.concatenate([f, jnp.zeros((members * LANES, LANES - fields), F32)], axis=1)
        f = f.T[:rows]
        own_ref[t] = f
        groups = [
            f[8 * g : 8 * g + 8, m * LANES : (m + 1) * LANES]
            for g in range(rows // 8)
            for m in range(members)
        ]
        sent_ref[t] = jnp.concatenate(groups, axis=0).astype(BF16)
        return carry

    lax.fori_loop(0, tiles, step, 0)


def column(row, rows):
    return jnp.broadcast_to(row, (LANES, LANES)).T[:rows]


def pad_row(ref, scratch, fields):
    scratch[...] = jnp.zeros_like(scratch)
    scratch[:, :fields] = ref[...]
    return scratch[...]


def slope_and_length(d):
    t = d * d + SMOOTH
    r = lax.rsqrt(t)
    return d * r, t * r


def near_kernel(own_ref, sib_ref, truth_ref, area_ref, shift_ref, coef_ref, acc_ref, loss_ref, goal, rpad, coefs, *, first, members, total):
    tiles, rows, _ = own_ref.shape
    fields = truth_ref.shape[0]
    c1 = (1.0 - (1.0 - ALPHA) / total) / (total - 1)
    c2 = (1.0 - (1.0 - ALPHA) / total) / (2.0 * total * (total - 1))

    here = slice(first * LANES, (first + tiles) * LANES)
    coefs[...] = column(pad_row(coef_ref, rpad, fields), rows)
    shifts = column(pad_row(shift_ref, rpad, fields), rows)
    goal[...] = jnp.zeros_like(goal)
    for t in range(tiles):
        at = slice((first + t) * LANES, (first + t + 1) * LANES)
        goal[t, :fields, :] = truth_ref[:, at] - shifts[:fields]
    loss_ref[...] = jnp.zeros_like(loss_ref)

    def step(t, carry):
        loss = jnp.zeros((8, LANES), F32)
        for g in range(rows // 8):
            span = slice(8 * g, 8 * g + 8)
            own = [own_ref[t, span, m * LANES : (m + 1) * LANES] for m in range(members)]
            sib = sib_ref[t, 8 * members * g : 8 * members * (g + 1), :].astype(F32)
            skill = jnp.zeros((8, LANES), F32)
            spread = jnp.zeros((8, LANES), F32)
            inner = jnp.zeros((8, LANES), F32)
            slopes = [jnp.zeros((8, LANES), F32) for _ in range(members)]
            for m in range(members):
                for n in range(m + 1, members):
                    a, b = slope_and_length(own[m] - own[n])
                    slopes[m] = slopes[m] + a
                    slopes[n] = slopes[n] - a
                    inner = inner + b
                for n in range(members):
                    a, b = slope_and_length(own[m] - sib[8 * n : 8 * n + 8])
                    slopes[m] = slopes[m] + a
                    spread = spread + b
            for m in range(members):
                a, b = slope_and_length(own[m] - goal[t, span, :])
                skill = skill + b
                acc_ref[t, span, m * LANES : (m + 1) * LANES] = a - c1 * slopes[m]
            loss = loss + coefs[span] * (skill * (1.0 / total) - c2 * (spread + 2.0 * inner))
        at = pl.multiple_of((first + t) * LANES, LANES)
        loss_ref[...] += loss * area_ref[:, pl.ds(at, LANES)]
        return carry

    lax.fori_loop(0, tiles, step, 0)


def far_kernel(*refs, first, before, members, total, fields):
    own_ref, far_ref, fwd_ref, acc_ref, area_ref, coef_ref, near_loss, x_hbm = refs[:8]
    earlier, refs = refs[8 : 8 + before], refs[8 + before :]
    grad_ref, dw_ref, bias_ref, loss_ref, rpad, coefs, grads, x, x_sem = refs
    tiles, rows, _ = own_ref.shape
    width = x.shape[3]
    span_all = members * LANES
    c1 = (1.0 - (1.0 - ALPHA) / total) / (total - 1)
    c2 = (1.0 - (1.0 - ALPHA) / total) / (2.0 * total * (total - 1))

    def fetch(t):
        points = pl.ds((first + t) * LANES, LANES)
        return pltpu.make_async_copy(x_hbm.at[:, points], x.at[t], x_sem.at[t])

    for t in range(tiles):
        fetch(t).start()
    coefs[...] = column(pad_row(coef_ref, rpad, fields), rows)
    grads[...] = jnp.zeros_like(grads)
    if before:
        bias_ref[...] = earlier[1][...]
        loss_ref[...] = earlier[2][...] + near_loss[...]
    else:
        bias_ref[...] = jnp.zeros_like(bias_ref)
        loss_ref[...] = near_loss[...]

    def step(t, carry):
        at = pl.multiple_of((first + t) * LANES, LANES)
        area = jnp.broadcast_to(area_ref[:, pl.ds(at, LANES)], (8, LANES))
        loss = jnp.zeros((8, LANES), F32)
        for g in range(rows // 8):
            span = slice(8 * g, 8 * g + 8)
            part = slice(8 * members * g, 8 * members * (g + 1))
            own = [own_ref[t, span, m * LANES : (m + 1) * LANES] for m in range(members)]
            far = far_ref[t, part, :].astype(F32)
            fwd = fwd_ref[t, part, :].astype(F32)
            spread = jnp.zeros((8, LANES), F32)
            scale = coefs[span] * area
            bias = jnp.zeros((8, LANES), F32)
            for m in range(members):
                slopes = jnp.zeros((8, LANES), F32)
                for other in (far, fwd):
                    for n in range(members):
                        a, b = slope_and_length(own[m] - other[8 * n : 8 * n + 8])
                        slopes = slopes + a
                        spread = spread + b
                here = slice(m * LANES, (m + 1) * LANES)
                grad = (scale * (acc_ref[t, span, here] - c1 * slopes)).astype(BF16).astype(F32)
                grads[t, span, here] = grad
                bias = bias + grad
            bias_ref[span, :] += bias
            loss = loss + coefs[span] * spread
        loss_ref[...] -= c2 * loss * area
        grad_ref[t] = grads[t].astype(BF16)
        return carry

    lax.fori_loop(0, tiles, step, 0)

    dw = earlier[0][...] if before else jnp.zeros(dw_ref.shape, F32)
    for t in range(tiles):
        fetch(t).wait()
        dw = dw + jnp.dot(grad_ref[t], x[t].reshape(span_all, width), preferred_element_type=F32)
    dw_ref[...] = dw


def pack_kernel(dw_ref, bias_ref, loss_ref, out_ref, padded, *, fields):
    padded[...] = jnp.zeros_like(padded)
    padded[: bias_ref.shape[0], :] = bias_ref[...]
    bias = jnp.sum(padded[...].T, axis=0, keepdims=True)
    loss = jnp.sum(jnp.sum(loss_ref[...], axis=0, keepdims=True), axis=1, keepdims=True)
    high = loss.astype(BF16).astype(F32)
    low = loss - high
    quarter = fields // 4
    lane = lax.broadcasted_iota(jnp.int32, (8, LANES), 1)
    row = lax.broadcasted_iota(jnp.int32, (8, LANES), 0) % 4
    bias = jnp.broadcast_to(bias, (8, LANES))
    extra = jnp.zeros((8, LANES), F32)
    for r in range(4):
        moved = pltpu.roll(bias, fields - quarter * r, 1)
        extra = jnp.where(row == r, moved, extra)
    extra = jnp.where(lane < fields + quarter, extra, 0.0)
    at = lane == fields + quarter
    extra = jnp.where(at & (row == 0), high, extra)
    extra = jnp.where(at & (row == 1), low, extra)
    table = dw_ref[...].T.reshape(-1, 8, LANES)
    keep = lax.broadcasted_iota(jnp.int32, table.shape, 2) < fields
    table = jnp.where(keep, table, extra[None])
    out_ref[...] = table.reshape(out_ref.shape).astype(BF16)


def slope_kernel(grad_ref, w_ref, out_ref):
    fields = w_ref.shape[0]
    s = lax.dot_general(
        grad_ref[0, :fields, :], w_ref[...], (((0,), (0,)), ((), ())), preferred_element_type=F32
    )
    out_ref[...] = s.astype(BF16).reshape(out_ref.shape)


def finish_kernel(parts_ref, dw_ref, bias_ref, loss_ref, *, fields, scale, count):
    parts = parts_ref[...].astype(F32).reshape(-1, 8, LANES)
    total = jnp.sum(parts, axis=0)
    total = total[:4] + total[4:]
    dw_ref[...] = total[:, :fields] * scale
    quarter = fields // 4
    lane = lax.broadcasted_iota(jnp.int32, (1, LANES), 1)
    bias = jnp.zeros((1, LANES), F32)
    for r in range(4):
        moved = pltpu.roll(total, (quarter * r - fields) % LANES, 1)[r : r + 1]
        bias = jnp.where((lane >= quarter * r) & (lane < quarter * (r + 1)), moved, bias)
    bias_ref[...] = bias[:, :fields] * scale
    at = fields + quarter
    loss_ref[...] = (total[0:1, at : at + 1] + total[1:2, at : at + 1]) * (1.0 / count)


def cost(us):
    return pl.CostEstimate(flops=int(us * 1e9), bytes_accessed=int(us * 3.5e6), transcendentals=0)


def shards(hidden, weights, shift, truth, area, coef):
    members, points, width = hidden.shape
    fields = weights.shape[1]
    total = members * lax.axis_size("member")
    all_points = points * lax.axis_size("point")
    rows = round_up(fields, 8)
    span = members * LANES
    weights, truth = weights.T, truth.T
    shift, coef, area = shift[None], coef[None], area[None]
    tile = lambda shape: pl.BlockSpec((1,) + shape, lambda i: (i, 0, 0))
    shape = jax.ShapeDtypeStruct
    vmem = pl.BlockSpec(memory_space=pltpu.VMEM)
    hbm = pl.BlockSpec(memory_space=pltpu.HBM)
    core_swap = [(0, 1), (1, 0), (2, 3), (3, 2)]
    chip_swap = [(0, 2), (1, 3), (2, 0), (3, 1)]

    def forecast(n, first, us):
        return pl.pallas_call(
            functools.partial(forecast_kernel, first=first),
            in_specs=[hbm, hbm],
            out_specs=[vmem, vmem],
            out_shape=[shape((n, rows, span), F32), shape((n, rows * members, LANES), BF16)],
            scratch_shapes=[
                pltpu.VMEM((n, members, LANES, width), BF16),
                pltpu.VMEM((fields, width), BF16),
                pltpu.SemaphoreType.DMA((n,)),
                pltpu.SemaphoreType.DMA,
            ],
            compiler_params=params(48 if first else 60),
            cost_estimate=cost(us),
            name="forecast",
        )(hidden, weights)

    def near(n, first, us, own, sib):
        return pl.pallas_call(
            functools.partial(near_kernel, first=first, members=members, total=total),
            in_specs=[vmem] * 6,
            out_specs=[vmem] * 2,
            out_shape=[shape((n, rows, span), F32), shape((8, LANES), F32)],
            scratch_shapes=[
                pltpu.VMEM((n, rows, LANES), F32),
                pltpu.VMEM((1, LANES), F32),
                pltpu.VMEM((rows, LANES), F32),
            ],
            compiler_params=params(),
            cost_estimate=cost(us),
            name="near",
        )(own, sib, truth, area, shift, coef)

    def far(n, first, us, own, away, fwd, acc, loss, *sums):
        return pl.pallas_call(
            functools.partial(
                far_kernel, first=first, before=len(sums), members=members, total=total, fields=fields
            ),
            in_specs=[vmem] * 7 + [hbm] + [vmem] * len(sums),
            out_specs=[vmem] * 4,
            out_shape=[
                shape((n, LANES, span), BF16),
                shape((LANES, width), F32),
                shape((rows, LANES), F32),
                shape((8, LANES), F32),
            ],
            scratch_shapes=[
                pltpu.VMEM((1, LANES), F32),
                pltpu.VMEM((rows, LANES), F32),
                pltpu.VMEM((n, LANES, span), F32),
                pltpu.VMEM((n, members, LANES, width), BF16),
                pltpu.SemaphoreType.DMA((n,)),
            ],
            compiler_params=params(),
            cost_estimate=cost(us),
            name="far",
        )(own, away, fwd, acc, area, coef, loss, hidden, *sums)

    across = lambda a: lax.ppermute(a, "member", chip_swap)
    beside = lambda a: lax.ppermute(a, "member", core_swap)
    hold = lax.optimization_barrier
    n0, n1, n2 = TILES
    a1, a2 = n0, n0 + n1
    own0, out0 = forecast(n0, 0, US[0])
    away0 = across(out0)
    own1, out1 = forecast(n1, a1, US[1])
    away1 = across(out1)
    own2, out2 = forecast(n2, a2, US[2])
    own0, out2 = hold((own0, out2))
    away2 = across(out2)
    sib0, sib1, sib2 = beside(out0), beside(out1), beside(out2)
    acc0, loss0 = near(n0, 0, US[3], own0, sib0)
    away0, acc0, own1 = hold((away0, acc0, own1))
    fwd0 = beside(away0)
    acc1, loss1 = near(n1, a1, US[4], own1, sib1)
    away1, acc1, acc0 = hold((away1, acc1, acc0))
    fwd1 = beside(away1)
    grad0, *sums = far(n0, 0, US[5], own0, away0, fwd0, acc0, loss0)
    grad1, *sums = far(n1, a1, US[6], own1, away1, fwd1, acc1, loss1, *sums)
    away2, own2, *sums = hold((away2, own2, *sums))
    fwd2 = beside(away2)
    acc2, loss2 = near(n2, a2, US[7], own2, sib2)
    grad2, *sums = far(n2, a2, US[8], own2, away2, fwd2, acc2, loss2, *sums)
    grads = [grad0, grad1, grad2]

    packed = pl.pallas_call(
        functools.partial(pack_kernel, fields=fields),
        out_shape=shape((width, LANES), BF16),
        scratch_shapes=[pltpu.VMEM((LANES, LANES), F32)],
        compiler_params=params(),
        name="pack",
    )(*sums)
    parts = lax.all_to_all(packed, ("member", "point"), split_axis=0, concat_axis=0, tiled=True)

    grad = grads[0] if len(grads) == 1 else jnp.concatenate(grads, axis=0)
    slope = pl.pallas_call(
        slope_kernel,
        grid=(points // LANES,),
        in_specs=[tile((LANES, span)), pl.BlockSpec((fields, width), lambda i: (0, 0))],
        out_specs=pl.BlockSpec((members, LANES, width), lambda i: (0, i, 0)),
        out_shape=shape(hidden.shape, BF16),
        compiler_params=params(),
        cost_estimate=cost(5),
        name="slope",
    )(grad, weights)

    own_rows = width // (lax.axis_size("member") * lax.axis_size("point"))
    dw, bias, loss = pl.pallas_call(
        functools.partial(
            finish_kernel, fields=fields, scale=float((total * all_points) ** -0.5), count=float(all_points * fields)
        ),
        out_shape=[shape((own_rows, fields), F32), shape((1, fields), F32), shape((1, 1), F32)],
        compiler_params=params(),
        name="finish",
    )(parts)
    return loss.reshape(()), slope, dw, bias.reshape(fields)


def solution(mesh):
    placed = (P("member", "point", None), P(), P(), P("point", None), P("point"), P())
    return jax.shard_map(
        shards,
        mesh=mesh,
        in_specs=placed,
        out_specs=(P(), P("member", "point", None), P(("member", "point"), None), P()),
        check_vma=False,
    )
```

```python
import functools

import jax
import jax.numpy as jnp
from jax import lax
from jax.experimental import pallas as pl
from jax.experimental.pallas import tpu as pltpu
from jax.sharding import PartitionSpec as P

F32 = jnp.float32
BF16 = jnp.bfloat16
LANES = 128
TILES = (2, 2, 2)
US = (.01,.01,.01,.01,8,8,.01,8,.01)
SMOOTH = 0.05 * 0.05
ALPHA = 0.95


def params(mib=48):
    return pltpu.CompilerParams(vmem_limit_bytes=mib * 1024 * 1024)


def round_up(n, k):
    return -(-n // k) * k


def forecast_kernel(x_hbm, w_hbm, x, own_ref, sent_ref, w, x_sems, w_sem, *, first):
    tiles, members, _, width = x.shape
    rows = own_ref.shape[1]
    fields = w.shape[0]
    w_copy = pltpu.make_async_copy(w_hbm, w, w_sem)
    w_copy.start()

    def fetch(t):
        points = pl.ds((first + t) * LANES, LANES)
        return pltpu.make_async_copy(x_hbm.at[:, points], x.at[t], x_sems.at[t])

    for t in range(tiles):
        fetch(t).start()
    w_copy.wait()

    def step(t, carry):
        fetch(t).wait()
        f = lax.dot_general(
            x[t].reshape(members * LANES, width),
            w[...],
            (((1,), (1,)), ((), ())),
            preferred_element_type=F32,
        )
        f = jnp.concatenate([f, jnp.zeros((members * LANES, LANES - fields), F32)], axis=1)
        f = f.T[:rows]
        own_ref[t] = f
        groups = [
            f[8 * g : 8 * g + 8, m * LANES : (m + 1) * LANES]
            for g in range(rows // 8)
            for m in range(members)
        ]
        sent_ref[t] = jnp.concatenate(groups, axis=0).astype(BF16)
        return carry

    lax.fori_loop(0, tiles, step, 0)


def column(row, rows):
    return jnp.broadcast_to(row, (LANES, LANES)).T[:rows]


def pad_row(ref, scratch, fields):
    scratch[...] = jnp.zeros_like(scratch)
    scratch[:, :fields] = ref[...]
    return scratch[...]


def slope_and_length(d):
    t = d * d + SMOOTH
    r = lax.rsqrt(t)
    return d * r, t * r


def near_kernel(own_ref, sib_ref, truth_ref, area_ref, shift_ref, coef_ref, acc_ref, loss_ref, goal, rpad, coefs, *, first, members, total):
    tiles, rows, _ = own_ref.shape
    fields = truth_ref.shape[0]
    c1 = (1.0 - (1.0 - ALPHA) / total) / (total - 1)
    c2 = (1.0 - (1.0 - ALPHA) / total) / (2.0 * total * (total - 1))

    here = slice(first * LANES, (first + tiles) * LANES)
    coefs[...] = column(pad_row(coef_ref, rpad, fields), rows)
    shifts = column(pad_row(shift_ref, rpad, fields), rows)
    goal[...] = jnp.zeros_like(goal)
    for t in range(tiles):
        at = slice((first + t) * LANES, (first + t + 1) * LANES)
        goal[t, :fields, :] = truth_ref[:, at] - shifts[:fields]
    loss_ref[...] = jnp.zeros_like(loss_ref)

    def step(t, carry):
        loss = jnp.zeros((8, LANES), F32)
        for g in range(rows // 8):
            span = slice(8 * g, 8 * g + 8)
            own = [own_ref[t, span, m * LANES : (m + 1) * LANES] for m in range(members)]
            sib = sib_ref[t, 8 * members * g : 8 * members * (g + 1), :].astype(F32)
            skill = jnp.zeros((8, LANES), F32)
            spread = jnp.zeros((8, LANES), F32)
            inner = jnp.zeros((8, LANES), F32)
            slopes = [jnp.zeros((8, LANES), F32) for _ in range(members)]
            for m in range(members):
                for n in range(m + 1, members):
                    a, b = slope_and_length(own[m] - own[n])
                    slopes[m] = slopes[m] + a
                    slopes[n] = slopes[n] - a
                    inner = inner + b
                for n in range(members):
                    a, b = slope_and_length(own[m] - sib[8 * n : 8 * n + 8])
                    slopes[m] = slopes[m] + a
                    spread = spread + b
            for m in range(members):
                a, b = slope_and_length(own[m] - goal[t, span, :])
                skill = skill + b
                acc_ref[t, span, m * LANES : (m + 1) * LANES] = a - c1 * slopes[m]
            loss = loss + coefs[span] * (skill * (1.0 / total) - c2 * (spread + 2.0 * inner))
        at = pl.multiple_of((first + t) * LANES, LANES)
        loss_ref[...] += loss * area_ref[:, pl.ds(at, LANES)]
        return carry

    lax.fori_loop(0, tiles, step, 0)


def pack(dw, bias_ref, loss_ref, padded, fields):
    padded[...] = jnp.zeros_like(padded)
    padded[: bias_ref.shape[0], :] = bias_ref[...]
    bias = jnp.sum(padded[...].T, axis=0, keepdims=True)
    loss = jnp.sum(jnp.sum(loss_ref[...], axis=0, keepdims=True), axis=1, keepdims=True)
    high = loss.astype(BF16).astype(F32)
    low = loss - high
    quarter = fields // 4
    lane = lax.broadcasted_iota(jnp.int32, (8, LANES), 1)
    row = lax.broadcasted_iota(jnp.int32, (8, LANES), 0) % 4
    bias = jnp.broadcast_to(bias, (8, LANES))
    extra = jnp.zeros((8, LANES), F32)
    for r in range(4):
        moved = pltpu.roll(bias, fields - quarter * r, 1)
        extra = jnp.where(row == r, moved, extra)
    extra = jnp.where(lane < fields + quarter, extra, 0.0)
    at = lane == fields + quarter
    extra = jnp.where(at & (row == 0), high, extra)
    extra = jnp.where(at & (row == 1), low, extra)
    table = dw.T.reshape(-1, 8, LANES)
    keep = lax.broadcasted_iota(jnp.int32, table.shape, 2) < fields
    table = jnp.where(keep, table, extra[None])
    return table.reshape(-1, LANES).astype(BF16)


def far_kernel(*refs, first, before, last, members, total, fields):
    own_ref, far_ref, fwd_ref, acc_ref, area_ref, coef_ref, near_loss, x = refs[:8]
    earlier, refs = refs[8 : 8 + before], refs[8 + before :]
    if last:
        grad_ref, out_ref, rpad, coefs, grads, bias_ref, loss_ref, padded = refs
    else:
        grad_ref, dw_ref, bias_ref, loss_ref, rpad, coefs, grads = refs
    tiles, rows, _ = own_ref.shape
    width = x.shape[3]
    span_all = members * LANES
    c1 = (1.0 - (1.0 - ALPHA) / total) / (total - 1)
    c2 = (1.0 - (1.0 - ALPHA) / total) / (2.0 * total * (total - 1))

    coefs[...] = column(pad_row(coef_ref, rpad, fields), rows)
    grads[...] = jnp.zeros_like(grads)
    if before:
        bias_ref[...] = earlier[1][...]
        loss_ref[...] = earlier[2][...] + near_loss[...]
    else:
        bias_ref[...] = jnp.zeros_like(bias_ref)
        loss_ref[...] = near_loss[...]

    def step(t, carry):
        at = pl.multiple_of((first + t) * LANES, LANES)
        area = jnp.broadcast_to(area_ref[:, pl.ds(at, LANES)], (8, LANES))
        loss = jnp.zeros((8, LANES), F32)
        for g in range(rows // 8):
            span = slice(8 * g, 8 * g + 8)
            part = slice(8 * members * g, 8 * members * (g + 1))
            own = [own_ref[t, span, m * LANES : (m + 1) * LANES] for m in range(members)]
            far = far_ref[t, part, :].astype(F32)
            fwd = fwd_ref[t, part, :].astype(F32)
            spread = jnp.zeros((8, LANES), F32)
            scale = coefs[span] * area
            bias = jnp.zeros((8, LANES), F32)
            for m in range(members):
                slopes = jnp.zeros((8, LANES), F32)
                for other in (far, fwd):
                    for n in range(members):
                        a, b = slope_and_length(own[m] - other[8 * n : 8 * n + 8])
                        slopes = slopes + a
                        spread = spread + b
                here = slice(m * LANES, (m + 1) * LANES)
                grad = (scale * (acc_ref[t, span, here] - c1 * slopes)).astype(BF16).astype(F32)
                grads[t, span, here] = grad
                bias = bias + grad
            bias_ref[span, :] += bias
            loss = loss + coefs[span] * spread
        loss_ref[...] -= c2 * loss * area
        grad_ref[t] = grads[t].astype(BF16)
        return carry

    lax.fori_loop(0, tiles, step, 0)

    dw = earlier[0][...] if before else jnp.zeros((LANES, width), F32)
    for t in range(tiles):
        dw = dw + jnp.dot(grad_ref[t], x[t].reshape(span_all, width), preferred_element_type=F32)
    if last:
        out_ref[...] = pack(dw, bias_ref, loss_ref, padded, fields)
    else:
        dw_ref[...] = dw


def slope_kernel(grad_ref, w_ref, out_ref):
    fields = w_ref.shape[0]
    s = lax.dot_general(
        grad_ref[0, :fields, :], w_ref[...], (((0,), (0,)), ((), ())), preferred_element_type=F32
    )
    out_ref[...] = s.astype(BF16).reshape(out_ref.shape)


def finish_kernel(parts_ref, dw_ref, bias_ref, loss_ref, *, fields, scale, count):
    parts = parts_ref[...].astype(F32).reshape(-1, 8, LANES)
    total = jnp.sum(parts, axis=0)
    total = total[:4] + total[4:]
    dw_ref[...] = total[:, :fields] * scale
    quarter = fields // 4
    lane = lax.broadcasted_iota(jnp.int32, (1, LANES), 1)
    bias = jnp.zeros((1, LANES), F32)
    for r in range(4):
        moved = pltpu.roll(total, (quarter * r - fields) % LANES, 1)[r : r + 1]
        bias = jnp.where((lane >= quarter * r) & (lane < quarter * (r + 1)), moved, bias)
    bias_ref[...] = bias[:, :fields] * scale
    at = fields + quarter
    loss_ref[...] = (total[0:1, at : at + 1] + total[1:2, at : at + 1]) * (1.0 / count)


def cost(us):
    return pl.CostEstimate(flops=int(us * 1e9), bytes_accessed=int(us * 3.5e6), transcendentals=0)


def shards(hidden, weights, shift, truth, area, coef):
    members, points, width = hidden.shape
    fields = weights.shape[1]
    total = members * lax.axis_size("member")
    all_points = points * lax.axis_size("point")
    rows = round_up(fields, 8)
    span = members * LANES
    weights, truth = weights.T, truth.T
    shift, coef, area = shift[None], coef[None], area[None]
    tile = lambda shape: pl.BlockSpec((1,) + shape, lambda i: (i, 0, 0))
    shape = jax.ShapeDtypeStruct
    vmem = pl.BlockSpec(memory_space=pltpu.VMEM)
    hbm = pl.BlockSpec(memory_space=pltpu.HBM)
    core_swap = [(0, 1), (1, 0), (2, 3), (3, 2)]
    chip_swap = [(0, 2), (1, 3), (2, 0), (3, 1)]

    def forecast(n, first, us):
        return pl.pallas_call(
            functools.partial(forecast_kernel, first=first),
            in_specs=[hbm, hbm],
            out_specs=[vmem] * 3,
            out_shape=[
                shape((n, members, LANES, width), BF16),
                shape((n, rows, span), F32),
                shape((n, rows * members, LANES), BF16),
            ],
            scratch_shapes=[
                pltpu.VMEM((fields, width), BF16),
                pltpu.SemaphoreType.DMA((n,)),
                pltpu.SemaphoreType.DMA,
            ],
            compiler_params=params(),
            cost_estimate=cost(us),
            name="forecast",
        )(hidden, pltpu.with_memory_space_constraint(weights, pltpu.HBM))

    def near(n, first, us, own, sib):
        return pl.pallas_call(
            functools.partial(near_kernel, first=first, members=members, total=total),
            in_specs=[vmem] * 6,
            out_specs=[vmem] * 2,
            out_shape=[shape((n, rows, span), F32), shape((8, LANES), F32)],
            scratch_shapes=[
                pltpu.VMEM((n, rows, LANES), F32),
                pltpu.VMEM((1, LANES), F32),
                pltpu.VMEM((rows, LANES), F32),
            ],
            compiler_params=params(),
            cost_estimate=cost(us),
            name="near",
        )(own, sib, truth, area, shift, coef)

    def far(n, first, us, own, away, fwd, acc, loss, x, *sums, last=False):
        sums_shapes = [((rows, LANES), F32), ((8, LANES), F32)]
        if last:
            outs = [shape((width, LANES), BF16)]
            extra = [pltpu.VMEM(*i) for i in sums_shapes] + [pltpu.VMEM((LANES, LANES), F32)]
        else:
            outs = [shape((LANES, width), F32)] + [shape(*i) for i in sums_shapes]
            extra = []
        return pl.pallas_call(
            functools.partial(
                far_kernel, first=first, before=len(sums), last=last, members=members, total=total, fields=fields
            ),
            in_specs=[vmem] * (8 + len(sums)),
            out_specs=[vmem] * (1 + len(outs)),
            out_shape=[shape((n, LANES, span), BF16)] + outs,
            scratch_shapes=[
                pltpu.VMEM((1, LANES), F32),
                pltpu.VMEM((rows, LANES), F32),
                pltpu.VMEM((n, LANES, span), F32),
            ]
            + extra,
            compiler_params=params(),
            cost_estimate=cost(us),
            name="far",
        )(own, away, fwd, acc, area, coef, loss, x, *sums)

    across = lambda a: lax.ppermute(a, "member", chip_swap)
    beside = lambda a: lax.ppermute(a, "member", core_swap)
    hold = lax.optimization_barrier
    n0, n1, n2 = TILES
    a1, a2 = n0, n0 + n1
    x0, own0, out0 = forecast(n0, 0, US[0])
    away0 = across(out0)
    x1, own1, out1 = forecast(n1, a1, US[1])
    away1 = across(out1)
    x2, own2, out2 = forecast(n2, a2, US[2])
    own0, out2 = hold((own0, out2))
    away2 = across(out2)
    sib0, sib1, sib2 = beside(out0), beside(out1), beside(out2)
    acc0, loss0 = near(n0, 0, US[3], own0, sib0)
    away0, acc0, own1 = hold((away0, acc0, own1))
    fwd0 = beside(away0)
    acc1, loss1 = near(n1, a1, US[4], own1, sib1)
    away1, acc1, acc0 = hold((away1, acc1, acc0))
    fwd1 = beside(away1)
    grad0, *sums = far(n0, 0, US[5], own0, away0, fwd0, acc0, loss0, x0)
    grad1, *sums = far(n1, a1, US[6], own1, away1, fwd1, acc1, loss1, x1, *sums)
    away2, own2, *sums = hold((away2, own2, *sums))
    fwd2 = beside(away2)
    acc2, loss2 = near(n2, a2, US[7], own2, sib2)
    grad2, packed = far(n2, a2, US[8], own2, away2, fwd2, acc2, loss2, x2, *sums, last=True)
    grads = [grad0, grad1, grad2]

    parts = lax.all_to_all(packed, ("member", "point"), split_axis=0, concat_axis=0, tiled=True)

    grad = grads[0] if len(grads) == 1 else jnp.concatenate(grads, axis=0)
    slope = pl.pallas_call(
        slope_kernel,
        grid=(points // LANES,),
        in_specs=[tile((LANES, span)), pl.BlockSpec((fields, width), lambda i: (0, 0))],
        out_specs=pl.BlockSpec((members, LANES, width), lambda i: (0, i, 0)),
        out_shape=shape(hidden.shape, BF16),
        compiler_params=params(),
        cost_estimate=cost(5),
        name="slope",
    )(grad, weights)

    own_rows = width // (lax.axis_size("member") * lax.axis_size("point"))
    dw, bias, loss = pl.pallas_call(
        functools.partial(
            finish_kernel, fields=fields, scale=float((total * all_points) ** -0.5), count=float(all_points * fields)
        ),
        out_shape=[shape((own_rows, fields), F32), shape((1, fields), F32), shape((1, 1), F32)],
        compiler_params=params(),
        name="finish",
    )(parts)
    return loss.reshape(()), slope, dw, bias.reshape(fields)


def solution(mesh):
    placed = (P("member", "point", None), P(), P(), P("point", None), P("point"), P())
    return jax.shard_map(
        shards,
        mesh=mesh,
        in_specs=placed,
        out_specs=(P(), P("member", "point", None), P(("member", "point"), None), P()),
        check_vma=False,
    )
```

```python
import functools

import jax
import jax.numpy as jnp
from jax import lax
from jax.experimental import pallas as pl
from jax.experimental.pallas import tpu as pltpu
from jax.sharding import PartitionSpec as P

F32 = jnp.float32
BF16 = jnp.bfloat16
LANES = 128
TILES = (2, 2, 2)
US = (.01,.01,.01,.01,8,8,.01,.01,.01,8)
SMOOTH = 0.05 * 0.05
ALPHA = 0.95


def params(mib=48):
    return pltpu.CompilerParams(vmem_limit_bytes=mib * 1024 * 1024)


def round_up(n, k):
    return -(-n // k) * k


def half_turn(a):
    return pltpu.roll(a, 4, 0)


def interleaved(f, members, fields):
    parts = lambda g: [f[8 * g : 8 * g + 8, m * LANES : (m + 1) * LANES] for m in range(members)]
    groups = [p for g in range(fields // 8) for p in parts(g)]
    ends = parts(fields // 8)
    groups += [ends[m] + half_turn(ends[m + 1]) for m in range(0, members, 2)]
    return jnp.concatenate(groups, axis=0).astype(BF16)


def others(ref, t, g, members, fields):
    count = members if 8 * g + 8 <= fields else members // 2
    block = ref[t, 8 * members * g : 8 * members * g + 8 * count, :].astype(F32)
    return [block[8 * n : 8 * n + 8] for n in range(count)]


def forecast_kernel(x_hbm, w_hbm, x, own_ref, sent_ref, w, x_sems, w_sem, *, first):
    tiles, members, _, width = x.shape
    rows = own_ref.shape[1]
    fields = w.shape[0]
    w_copy = pltpu.make_async_copy(w_hbm, w, w_sem)
    w_copy.start()

    def fetch(t):
        points = pl.ds((first + t) * LANES, LANES)
        return pltpu.make_async_copy(x_hbm.at[:, points], x.at[t], x_sems.at[t])

    for t in range(tiles):
        fetch(t).start()
    w_copy.wait()

    def step(t, carry):
        fetch(t).wait()
        f = lax.dot_general(
            x[t].reshape(members * LANES, width),
            w[...],
            (((1,), (1,)), ((), ())),
            preferred_element_type=F32,
        )
        f = jnp.concatenate([f, jnp.zeros((members * LANES, LANES - fields), F32)], axis=1)
        f = f.T[:rows]
        own_ref[t] = f
        sent_ref[t] = interleaved(f, members, fields)
        return carry

    lax.fori_loop(0, tiles, step, 0)


def column(row, rows):
    return jnp.broadcast_to(row, (LANES, LANES)).T[:rows]


def pad_row(ref, scratch, fields):
    scratch[...] = jnp.zeros_like(scratch)
    scratch[:, :fields] = ref[...]
    return scratch[...]


def slope_and_length(d):
    t = d * d + SMOOTH
    r = lax.rsqrt(t)
    return d * r, t * r


def near_kernel(own_ref, sib_ref, truth_ref, area_ref, shift_ref, coef_ref, acc_ref, loss_ref, goal, rpad, coefs, *, first, members, total):
    tiles, rows, _ = own_ref.shape
    fields = truth_ref.shape[0]
    c1 = (1.0 - (1.0 - ALPHA) / total) / (total - 1)
    c2 = (1.0 - (1.0 - ALPHA) / total) / (2.0 * total * (total - 1))

    here = slice(first * LANES, (first + tiles) * LANES)
    coefs[...] = column(pad_row(coef_ref, rpad, fields), rows)
    shifts = column(pad_row(shift_ref, rpad, fields), rows)
    goal[...] = jnp.zeros_like(goal)
    for t in range(tiles):
        at = slice((first + t) * LANES, (first + t + 1) * LANES)
        goal[t, :fields, :] = truth_ref[:, at] - shifts[:fields]
    loss_ref[...] = jnp.zeros_like(loss_ref)

    def step(t, carry):
        loss = jnp.zeros((8, LANES), F32)
        for g in range(rows // 8):
            span = slice(8 * g, 8 * g + 8)
            own = [own_ref[t, span, m * LANES : (m + 1) * LANES] for m in range(members)]
            sib = others(sib_ref, t, g, members, fields)
            folded = len(sib) < members
            skill = jnp.zeros((8, LANES), F32)
            spread = jnp.zeros((8, LANES), F32)
            inner = jnp.zeros((8, LANES), F32)
            slopes = [jnp.zeros((8, LANES), F32) for _ in range(members)]
            for m in range(members):
                mine = own[m] + half_turn(own[m]) if folded else own[m]
                for other in sib:
                    a, b = slope_and_length(mine - other)
                    slopes[m] = slopes[m] + a
                    spread = spread + b
                if folded:
                    slopes[m] = slopes[m] + half_turn(slopes[m])
            if folded:
                spread = spread + half_turn(spread)
            for m in range(members):
                for n in range(m + 1, members):
                    a, b = slope_and_length(own[m] - own[n])
                    slopes[m] = slopes[m] + a
                    slopes[n] = slopes[n] - a
                    inner = inner + b
            for m in range(members):
                a, b = slope_and_length(own[m] - goal[t, span, :])
                skill = skill + b
                acc_ref[t, span, m * LANES : (m + 1) * LANES] = a - c1 * slopes[m]
            loss = loss + coefs[span] * (skill * (1.0 / total) - c2 * (spread + 2.0 * inner))
        at = pl.multiple_of((first + t) * LANES, LANES)
        loss_ref[...] += loss * area_ref[:, pl.ds(at, LANES)]
        return carry

    lax.fori_loop(0, tiles, step, 0)


def direct_kernel(own_ref, far_ref, acc_ref, loss_in, area_ref, coef_ref, out_ref, loss_ref, rpad, coefs, *, first, members, total):
    tiles, rows, _ = own_ref.shape
    fields = coef_ref.shape[1]
    c1 = (1.0 - (1.0 - ALPHA) / total) / (total - 1)
    c2 = (1.0 - (1.0 - ALPHA) / total) / (2.0 * total * (total - 1))
    coefs[...] = column(pad_row(coef_ref, rpad, fields), rows)
    loss_ref[...] = loss_in[...]

    def step(t, carry):
        loss = jnp.zeros((8, LANES), F32)
        for g in range(rows // 8):
            span = slice(8 * g, 8 * g + 8)
            own = [own_ref[t, span, m * LANES : (m + 1) * LANES] for m in range(members)]
            remote = others(far_ref, t, g, members, fields)
            folded = len(remote) < members
            spread = jnp.zeros((8, LANES), F32)
            for m in range(members):
                mine = own[m] + half_turn(own[m]) if folded else own[m]
                slopes = jnp.zeros((8, LANES), F32)
                for other in remote:
                    a, b = slope_and_length(mine - other)
                    slopes = slopes + a
                    spread = spread + b
                if folded:
                    slopes = slopes + half_turn(slopes)
                here = slice(m * LANES, (m + 1) * LANES)
                out_ref[t, span, here] = acc_ref[t, span, here] - c1 * slopes
            if folded:
                spread = spread + half_turn(spread)
            loss = loss + coefs[span] * spread
        at = pl.multiple_of((first + t) * LANES, LANES)
        loss_ref[...] -= c2 * loss * area_ref[:, pl.ds(at, LANES)]
        return carry

    lax.fori_loop(0, tiles, step, 0)


def pack(dw, bias_ref, loss_ref, padded, fields):
    padded[...] = jnp.zeros_like(padded)
    padded[: bias_ref.shape[0], :] = bias_ref[...]
    bias = jnp.sum(padded[...].T, axis=0, keepdims=True)
    loss = jnp.sum(jnp.sum(loss_ref[...], axis=0, keepdims=True), axis=1, keepdims=True)
    high = loss.astype(BF16).astype(F32)
    low = loss - high
    quarter = fields // 4
    lane = lax.broadcasted_iota(jnp.int32, (8, LANES), 1)
    row = lax.broadcasted_iota(jnp.int32, (8, LANES), 0) % 4
    bias = jnp.broadcast_to(bias, (8, LANES))
    extra = jnp.zeros((8, LANES), F32)
    for r in range(4):
        moved = pltpu.roll(bias, fields - quarter * r, 1)
        extra = jnp.where(row == r, moved, extra)
    extra = jnp.where(lane < fields + quarter, extra, 0.0)
    at = lane == fields + quarter
    extra = jnp.where(at & (row == 0), high, extra)
    extra = jnp.where(at & (row == 1), low, extra)
    table = dw.T.reshape(-1, 8, LANES)
    keep = lax.broadcasted_iota(jnp.int32, table.shape, 2) < fields
    table = jnp.where(keep, table, extra[None])
    return table.reshape(-1, LANES).astype(BF16)


def far_kernel(*refs, first, before, received, last, members, total, fields):
    own_ref, acc_ref, area_ref, coef_ref, near_loss, x = refs[:6]
    earlier, refs = refs[6 : 6 + before], refs[6 + before :]
    sources, refs = refs[:received], refs[received:]
    if last:
        grad_ref, out_ref, rpad, coefs, grads, bias_ref, loss_ref, padded = refs
    else:
        grad_ref, dw_ref, bias_ref, loss_ref, rpad, coefs, grads = refs
    tiles, rows, _ = own_ref.shape
    width = x.shape[3]
    span_all = members * LANES
    c1 = (1.0 - (1.0 - ALPHA) / total) / (total - 1)
    c2 = (1.0 - (1.0 - ALPHA) / total) / (2.0 * total * (total - 1))

    coefs[...] = column(pad_row(coef_ref, rpad, fields), rows)
    grads[...] = jnp.zeros_like(grads)
    if before:
        bias_ref[...] = earlier[1][...]
        loss_ref[...] = earlier[2][...] + near_loss[...]
    else:
        bias_ref[...] = jnp.zeros_like(bias_ref)
        loss_ref[...] = near_loss[...]

    def step(t, carry):
        at = pl.multiple_of((first + t) * LANES, LANES)
        area = jnp.broadcast_to(area_ref[:, pl.ds(at, LANES)], (8, LANES))
        loss = jnp.zeros((8, LANES), F32)
        for g in range(rows // 8):
            span = slice(8 * g, 8 * g + 8)
            own = [own_ref[t, span, m * LANES : (m + 1) * LANES] for m in range(members)]
            remote = [o for ref in sources for o in others(ref, t, g, members, fields)]
            folded = len(remote) < received * members
            spread = jnp.zeros((8, LANES), F32)
            scale = coefs[span] * area
            bias = jnp.zeros((8, LANES), F32)
            for m in range(members):
                mine = own[m] + half_turn(own[m]) if folded else own[m]
                slopes = jnp.zeros((8, LANES), F32)
                for other in remote:
                    a, b = slope_and_length(mine - other)
                    slopes = slopes + a
                    spread = spread + b
                if folded:
                    slopes = slopes + half_turn(slopes)
                here = slice(m * LANES, (m + 1) * LANES)
                grad = (scale * (acc_ref[t, span, here] - c1 * slopes)).astype(BF16).astype(F32)
                grads[t, span, here] = grad
                bias = bias + grad
            if folded:
                spread = spread + half_turn(spread)
            bias_ref[span, :] += bias
            loss = loss + coefs[span] * spread
        loss_ref[...] -= c2 * loss * area
        grad_ref[t] = grads[t].astype(BF16)
        return carry

    lax.fori_loop(0, tiles, step, 0)

    dw = earlier[0][...] if before else jnp.zeros((LANES, width), F32)
    for t in range(tiles):
        dw = dw + jnp.dot(grad_ref[t], x[t].reshape(span_all, width), preferred_element_type=F32)
    if last:
        out_ref[...] = pack(dw, bias_ref, loss_ref, padded, fields)
    else:
        dw_ref[...] = dw


def slope_kernel(grad_ref, w_ref, out_ref):
    fields = w_ref.shape[0]
    s = lax.dot_general(
        grad_ref[0, :fields, :], w_ref[...], (((0,), (0,)), ((), ())), preferred_element_type=F32
    )
    out_ref[...] = s.astype(BF16).reshape(out_ref.shape)


def finish_kernel(parts_ref, dw_ref, bias_ref, loss_ref, *, fields, scale, count):
    parts = parts_ref[...].astype(F32).reshape(-1, 8, LANES)
    total = jnp.sum(parts, axis=0)
    total = total[:4] + total[4:]
    dw_ref[...] = total[:, :fields] * scale
    quarter = fields // 4
    lane = lax.broadcasted_iota(jnp.int32, (1, LANES), 1)
    bias = jnp.zeros((1, LANES), F32)
    for r in range(4):
        moved = pltpu.roll(total, (quarter * r - fields) % LANES, 1)[r : r + 1]
        bias = jnp.where((lane >= quarter * r) & (lane < quarter * (r + 1)), moved, bias)
    bias_ref[...] = bias[:, :fields] * scale
    at = fields + quarter
    loss_ref[...] = (total[0:1, at : at + 1] + total[1:2, at : at + 1]) * (1.0 / count)


def cost(us):
    return pl.CostEstimate(flops=int(us * 1e9), bytes_accessed=int(us * 3.5e6), transcendentals=0)


def shards(hidden, weights, shift, truth, area, coef):
    members, points, width = hidden.shape
    fields = weights.shape[1]
    total = members * lax.axis_size("member")
    all_points = points * lax.axis_size("point")
    rows = round_up(fields, 8)
    span = members * LANES
    sent_rows = members * fields
    weights, truth = weights.T, truth.T
    shift, coef, area = shift[None], coef[None], area[None]
    tile = lambda shape: pl.BlockSpec((1,) + shape, lambda i: (i, 0, 0))
    shape = jax.ShapeDtypeStruct
    vmem = pl.BlockSpec(memory_space=pltpu.VMEM)
    hbm = pl.BlockSpec(memory_space=pltpu.HBM)
    core_swap = [(0, 1), (1, 0), (2, 3), (3, 2)]
    chip_swap = [(0, 2), (1, 3), (2, 0), (3, 1)]

    def forecast(n, first, us):
        return pl.pallas_call(
            functools.partial(forecast_kernel, first=first),
            in_specs=[hbm, hbm],
            out_specs=[vmem] * 3,
            out_shape=[
                shape((n, members, LANES, width), BF16),
                shape((n, rows, span), F32),
                shape((n, sent_rows, LANES), BF16),
            ],
            scratch_shapes=[
                pltpu.VMEM((fields, width), BF16),
                pltpu.SemaphoreType.DMA((n,)),
                pltpu.SemaphoreType.DMA,
            ],
            compiler_params=params(),
            cost_estimate=cost(us),
            name="forecast",
        )(hidden, pltpu.with_memory_space_constraint(weights, pltpu.HBM))

    def near(n, first, us, own, sib):
        return pl.pallas_call(
            functools.partial(near_kernel, first=first, members=members, total=total),
            in_specs=[vmem] * 6,
            out_specs=[vmem] * 2,
            out_shape=[shape((n, rows, span), F32), shape((8, LANES), F32)],
            scratch_shapes=[
                pltpu.VMEM((n, rows, LANES), F32),
                pltpu.VMEM((1, LANES), F32),
                pltpu.VMEM((rows, LANES), F32),
            ],
            compiler_params=params(),
            cost_estimate=cost(us),
            name="near",
        )(own, sib, truth, area, shift, coef)

    def direct(n, first, us, own, away, acc, loss):
        return pl.pallas_call(
            functools.partial(direct_kernel, first=first, members=members, total=total),
            in_specs=[vmem] * 6,
            out_specs=[vmem] * 2,
            out_shape=[shape((n, rows, span), F32), shape((8, LANES), F32)],
            scratch_shapes=[pltpu.VMEM((1, LANES), F32), pltpu.VMEM((rows, LANES), F32)],
            compiler_params=params(),
            cost_estimate=cost(us),
            name="direct",
        )(own, away, acc, loss, area, coef)

    def far(n, first, us, own, acc, loss, x, *sums, received, last=False):
        sums_shapes = [((rows, LANES), F32), ((8, LANES), F32)]
        if last:
            outs = [shape((width, LANES), BF16)]
            extra = [pltpu.VMEM(*i) for i in sums_shapes] + [pltpu.VMEM((LANES, LANES), F32)]
        else:
            outs = [shape((LANES, width), F32)] + [shape(*i) for i in sums_shapes]
            extra = []
        return pl.pallas_call(
            functools.partial(
                far_kernel, first=first, before=len(sums), received=len(received), last=last, members=members, total=total, fields=fields
            ),
            in_specs=[vmem] * (6 + len(sums) + len(received)),
            out_specs=[vmem] * (1 + len(outs)),
            out_shape=[shape((n, LANES, span), BF16)] + outs,
            scratch_shapes=[
                pltpu.VMEM((1, LANES), F32),
                pltpu.VMEM((rows, LANES), F32),
                pltpu.VMEM((n, LANES, span), F32),
            ]
            + extra,
            compiler_params=params(),
            cost_estimate=cost(us),
            name="far",
        )(own, acc, area, coef, loss, x, *sums, *received)

    across = lambda a: lax.ppermute(a, "member", chip_swap)
    beside = lambda a: lax.ppermute(a, "member", core_swap)
    hold = lax.optimization_barrier
    n0, n1, n2 = TILES
    a1, a2 = n0, n0 + n1
    x0, own0, out0 = forecast(n0, 0, US[0])
    away0 = across(out0)
    x1, own1, out1 = forecast(n1, a1, US[1])
    away1 = across(out1)
    x2, own2, out2 = forecast(n2, a2, US[2])
    own0, out2 = hold((own0, out2))
    away2 = across(out2)
    sib0, sib1, sib2 = beside(out0), beside(out1), beside(out2)
    acc0, loss0 = near(n0, 0, US[3], own0, sib0)
    away0, acc0, own1, own2 = hold((away0, acc0, own1, own2))
    fwd0 = beside(away0)
    acc1, loss1 = near(n1, a1, US[4], own1, sib1)
    acc2, loss2 = near(n2, a2, US[7], own2, sib2)
    away1, acc1, acc0, acc2 = hold((away1, acc1, acc0, acc2))
    fwd1 = beside(away1)
    grad0, *sums = far(n0, 0, US[5], own0, acc0, loss0, x0, received=(away0, fwd0))
    grad1, *sums = far(n1, a1, US[6], own1, acc1, loss1, x1, *sums, received=(away1, fwd1))
    away2, acc2, *sums = hold((away2, acc2, *sums))
    fwd2 = beside(away2)
    acc2, loss2 = direct(n2, a2, US[9], own2, away2, acc2, loss2)
    grad2, packed = far(n2, a2, US[8], own2, acc2, loss2, x2, *sums, received=(fwd2,), last=True)
    grads = [grad0, grad1, grad2]

    parts = lax.all_to_all(packed, ("member", "point"), split_axis=0, concat_axis=0, tiled=True)

    grad = grads[0] if len(grads) == 1 else jnp.concatenate(grads, axis=0)
    slope = pl.pallas_call(
        slope_kernel,
        grid=(points // LANES,),
        in_specs=[tile((LANES, span)), pl.BlockSpec((fields, width), lambda i: (0, 0))],
        out_specs=pl.BlockSpec((members, LANES, width), lambda i: (0, i, 0)),
        out_shape=shape(hidden.shape, BF16),
        compiler_params=params(),
        cost_estimate=cost(5),
        name="slope",
    )(grad, weights)

    own_rows = width // (lax.axis_size("member") * lax.axis_size("point"))
    dw, bias, loss = pl.pallas_call(
        functools.partial(
            finish_kernel, fields=fields, scale=float((total * all_points) ** -0.5), count=float(all_points * fields)
        ),
        out_shape=[shape((own_rows, fields), F32), shape((1, fields), F32), shape((1, 1), F32)],
        compiler_params=params(),
        name="finish",
    )(parts)
    return loss.reshape(()), slope, dw, bias.reshape(fields)


def solution(mesh):
    placed = (P("member", "point", None), P(), P(), P("point", None), P("point"), P())
    return jax.shard_map(
        shards,
        mesh=mesh,
        in_specs=placed,
        out_specs=(P(), P("member", "point", None), P(("member", "point"), None), P()),
        check_vma=False,
    )
```

```python
import functools

import jax
import jax.numpy as jnp
from jax import lax
from jax.experimental import pallas as pl
from jax.experimental.pallas import tpu as pltpu
from jax.sharding import PartitionSpec as P

F32 = jnp.float32
BF16 = jnp.bfloat16
LANES = 128
TILES = (2, 2, 2)
US = (.01,.01,.01,.01,8,8,.01,.01,.01,8)
SMOOTH = 0.05 * 0.05
ALPHA = 0.95


def params(mib=48):
    return pltpu.CompilerParams(vmem_limit_bytes=mib * 1024 * 1024)


def round_up(n, k):
    return -(-n // k) * k


def half_turn(a):
    return pltpu.roll(a, 4, 0)


def interleaved(f, members, fields):
    parts = lambda g: [f[8 * g : 8 * g + 8, m * LANES : (m + 1) * LANES] for m in range(members)]
    groups = [p for g in range(fields // 8) for p in parts(g)]
    ends = parts(fields // 8)
    groups += [ends[m] + half_turn(ends[m + 1]) for m in range(0, members, 2)]
    return jnp.concatenate(groups, axis=0).astype(BF16)


def others(ref, t, g, members, fields):
    count = members if 8 * g + 8 <= fields else members // 2
    block = ref[t, 8 * members * g : 8 * members * g + 8 * count, :].astype(F32)
    return [block[8 * n : 8 * n + 8] for n in range(count)]


def forecast_kernel(x_hbm, w_hbm, x, own_ref, sent_ref, w, x_sems, w_sem, *, first):
    tiles, members, _, width = x.shape
    rows = own_ref.shape[1]
    fields = w.shape[0]
    w_copy = pltpu.make_async_copy(w_hbm, w, w_sem)
    w_copy.start()

    def fetch(t):
        points = pl.ds((first + t) * LANES, LANES)
        return pltpu.make_async_copy(x_hbm.at[:, points], x.at[t], x_sems.at[t])

    for t in range(tiles):
        fetch(t).start()
    w_copy.wait()

    def step(t, carry):
        fetch(t).wait()
        f = lax.dot_general(
            x[t].reshape(members * LANES, width),
            w[...],
            (((1,), (1,)), ((), ())),
            preferred_element_type=F32,
        )
        f = jnp.concatenate([f, jnp.zeros((members * LANES, LANES - fields), F32)], axis=1)
        f = f.T[:rows]
        own_ref[t] = f
        sent_ref[t] = interleaved(f, members, fields)
        return carry

    lax.fori_loop(0, tiles, step, 0)


def column(row, rows):
    return jnp.broadcast_to(row, (LANES, LANES)).T[:rows]


def pad_row(ref, scratch, fields):
    scratch[...] = jnp.zeros_like(scratch)
    scratch[:, :fields] = ref[...]
    return scratch[...]


def slope_and_length(d):
    t = d * d + SMOOTH
    r = lax.rsqrt(t)
    return d * r, t * r


def near_kernel(own_ref, sib_ref, truth_ref, area_ref, shift_ref, coef_ref, acc_ref, loss_ref, coefs, goal, rpad, *, first, members, total):
    tiles, rows, _ = own_ref.shape
    fields = truth_ref.shape[0]
    c1 = (1.0 - (1.0 - ALPHA) / total) / (total - 1)
    c2 = (1.0 - (1.0 - ALPHA) / total) / (2.0 * total * (total - 1))

    here = slice(first * LANES, (first + tiles) * LANES)
    coefs[...] = column(pad_row(coef_ref, rpad, fields), rows)
    shifts = column(pad_row(shift_ref, rpad, fields), rows)
    goal[...] = jnp.zeros_like(goal)
    for t in range(tiles):
        at = slice((first + t) * LANES, (first + t + 1) * LANES)
        goal[t, :fields, :] = truth_ref[:, at] - shifts[:fields]
    loss_ref[...] = jnp.zeros_like(loss_ref)

    def step(t, carry):
        loss = jnp.zeros((8, LANES), F32)
        for g in range(rows // 8):
            span = slice(8 * g, 8 * g + 8)
            own = [own_ref[t, span, m * LANES : (m + 1) * LANES] for m in range(members)]
            sib = others(sib_ref, t, g, members, fields)
            folded = len(sib) < members
            skill = jnp.zeros((8, LANES), F32)
            spread = jnp.zeros((8, LANES), F32)
            inner = jnp.zeros((8, LANES), F32)
            slopes = [jnp.zeros((8, LANES), F32) for _ in range(members)]
            for m in range(members):
                mine = own[m] + half_turn(own[m]) if folded else own[m]
                for other in sib:
                    a, b = slope_and_length(mine - other)
                    slopes[m] = slopes[m] + a
                    spread = spread + b
                if folded:
                    slopes[m] = slopes[m] + half_turn(slopes[m])
            if folded:
                spread = spread + half_turn(spread)
            for m in range(members):
                for n in range(m + 1, members):
                    a, b = slope_and_length(own[m] - own[n])
                    slopes[m] = slopes[m] + a
                    slopes[n] = slopes[n] - a
                    inner = inner + b
            for m in range(members):
                a, b = slope_and_length(own[m] - goal[t, span, :])
                skill = skill + b
                acc_ref[t, span, m * LANES : (m + 1) * LANES] = a - c1 * slopes[m]
            loss = loss + coefs[span] * (skill * (1.0 / total) - c2 * (spread + 2.0 * inner))
        at = pl.multiple_of((first + t) * LANES, LANES)
        loss_ref[...] += loss * area_ref[:, pl.ds(at, LANES)]
        return carry

    lax.fori_loop(0, tiles, step, 0)


def direct_kernel(own_ref, far_ref, acc_ref, loss_in, area_ref, coefs, out_ref, loss_ref, *, first, members, total, fields):
    tiles, rows, _ = own_ref.shape
    c1 = (1.0 - (1.0 - ALPHA) / total) / (total - 1)
    c2 = (1.0 - (1.0 - ALPHA) / total) / (2.0 * total * (total - 1))
    loss_ref[...] = loss_in[...]

    def step(t, carry):
        loss = jnp.zeros((8, LANES), F32)
        for g in range(rows // 8):
            span = slice(8 * g, 8 * g + 8)
            own = [own_ref[t, span, m * LANES : (m + 1) * LANES] for m in range(members)]
            remote = others(far_ref, t, g, members, fields)
            folded = len(remote) < members
            spread = jnp.zeros((8, LANES), F32)
            for m in range(members):
                mine = own[m] + half_turn(own[m]) if folded else own[m]
                slopes = jnp.zeros((8, LANES), F32)
                for other in remote:
                    a, b = slope_and_length(mine - other)
                    slopes = slopes + a
                    spread = spread + b
                if folded:
                    slopes = slopes + half_turn(slopes)
                here = slice(m * LANES, (m + 1) * LANES)
                out_ref[t, span, here] = acc_ref[t, span, here] - c1 * slopes
            if folded:
                spread = spread + half_turn(spread)
            loss = loss + coefs[span] * spread
        at = pl.multiple_of((first + t) * LANES, LANES)
        loss_ref[...] -= c2 * loss * area_ref[:, pl.ds(at, LANES)]
        return carry

    lax.fori_loop(0, tiles, step, 0)


def pack(dw, bias_ref, loss_ref, padded, fields):
    padded[...] = jnp.zeros_like(padded)
    padded[: bias_ref.shape[0], :] = bias_ref[...]
    bias = jnp.sum(padded[...].T, axis=0, keepdims=True)
    loss = jnp.sum(jnp.sum(loss_ref[...], axis=0, keepdims=True), axis=1, keepdims=True)
    high = loss.astype(BF16).astype(F32)
    low = loss - high
    quarter = fields // 4
    lane = lax.broadcasted_iota(jnp.int32, (8, LANES), 1)
    row = lax.broadcasted_iota(jnp.int32, (8, LANES), 0) % 4
    bias = jnp.broadcast_to(bias, (8, LANES))
    extra = jnp.zeros((8, LANES), F32)
    for r in range(4):
        moved = pltpu.roll(bias, fields - quarter * r, 1)
        extra = jnp.where(row == r, moved, extra)
    extra = jnp.where(lane < fields + quarter, extra, 0.0)
    at = lane == fields + quarter
    extra = jnp.where(at & (row == 0), high, extra)
    extra = jnp.where(at & (row == 1), low, extra)
    table = dw.T.reshape(-1, 8, LANES)
    keep = lax.broadcasted_iota(jnp.int32, table.shape, 2) < fields
    table = jnp.where(keep, table, extra[None])
    return table.reshape(-1, LANES).astype(BF16)


def far_kernel(*refs, first, before, received, last, members, total, fields):
    own_ref, acc_ref, area_ref, coefs, near_loss, x = refs[:6]
    earlier, refs = refs[6 : 6 + before], refs[6 + before :]
    sources, refs = refs[:received], refs[received:]
    if last:
        grad_ref, out_ref, grads, bias_ref, loss_ref, padded = refs
    else:
        grad_ref, dw_ref, bias_ref, loss_ref, grads = refs
    tiles, rows, _ = own_ref.shape
    width = x.shape[3]
    span_all = members * LANES
    c1 = (1.0 - (1.0 - ALPHA) / total) / (total - 1)
    c2 = (1.0 - (1.0 - ALPHA) / total) / (2.0 * total * (total - 1))

    grads[:, rows:, :] = jnp.zeros((tiles, LANES - rows, span_all), F32)
    if before:
        bias_ref[...] = earlier[1][...]
        loss_ref[...] = earlier[2][...] + near_loss[...]
    else:
        bias_ref[...] = jnp.zeros_like(bias_ref)
        loss_ref[...] = near_loss[...]

    def step(t, carry):
        at = pl.multiple_of((first + t) * LANES, LANES)
        area = jnp.broadcast_to(area_ref[:, pl.ds(at, LANES)], (8, LANES))
        loss = jnp.zeros((8, LANES), F32)
        for g in range(rows // 8):
            span = slice(8 * g, 8 * g + 8)
            own = [own_ref[t, span, m * LANES : (m + 1) * LANES] for m in range(members)]
            remote = [o for ref in sources for o in others(ref, t, g, members, fields)]
            folded = len(remote) < received * members
            spread = jnp.zeros((8, LANES), F32)
            scale = coefs[span] * area
            bias = jnp.zeros((8, LANES), F32)
            for m in range(members):
                mine = own[m] + half_turn(own[m]) if folded else own[m]
                slopes = jnp.zeros((8, LANES), F32)
                for other in remote:
                    a, b = slope_and_length(mine - other)
                    slopes = slopes + a
                    spread = spread + b
                if folded:
                    slopes = slopes + half_turn(slopes)
                here = slice(m * LANES, (m + 1) * LANES)
                grad = (scale * (acc_ref[t, span, here] - c1 * slopes)).astype(BF16).astype(F32)
                grads[t, span, here] = grad
                bias = bias + grad
            if folded:
                spread = spread + half_turn(spread)
            bias_ref[span, :] += bias
            loss = loss + coefs[span] * spread
        loss_ref[...] -= c2 * loss * area
        grad_ref[t] = grads[t].astype(BF16)
        return carry

    lax.fori_loop(0, tiles, step, 0)

    dw = earlier[0][...] if before else jnp.zeros((LANES, width), F32)
    for t in range(tiles):
        dw = dw + jnp.dot(grad_ref[t], x[t].reshape(span_all, width), preferred_element_type=F32)
    if last:
        out_ref[...] = pack(dw, bias_ref, loss_ref, padded, fields)
    else:
        dw_ref[...] = dw


def slope_kernel(grad_ref, w_ref, out_ref):
    fields = w_ref.shape[0]
    s = lax.dot_general(
        grad_ref[0, :fields, :], w_ref[...], (((0,), (0,)), ((), ())), preferred_element_type=F32
    )
    out_ref[...] = s.astype(BF16).reshape(out_ref.shape)


def finish_kernel(parts_ref, dw_ref, bias_ref, loss_ref, *, fields, scale, count):
    parts = parts_ref[...].astype(F32).reshape(-1, 8, LANES)
    total = jnp.sum(parts, axis=0)
    total = total[:4] + total[4:]
    dw_ref[...] = total[:, :fields] * scale
    quarter = fields // 4
    lane = lax.broadcasted_iota(jnp.int32, (1, LANES), 1)
    bias = jnp.zeros((1, LANES), F32)
    for r in range(4):
        moved = pltpu.roll(total, (quarter * r - fields) % LANES, 1)[r : r + 1]
        bias = jnp.where((lane >= quarter * r) & (lane < quarter * (r + 1)), moved, bias)
    bias_ref[...] = bias[:, :fields] * scale
    at = fields + quarter
    loss_ref[...] = (total[0:1, at : at + 1] + total[1:2, at : at + 1]) * (1.0 / count)


def cost(us):
    return pl.CostEstimate(flops=int(us * 1e9), bytes_accessed=int(us * 3.5e6), transcendentals=0)


def shards(hidden, weights, shift, truth, area, coef):
    members, points, width = hidden.shape
    fields = weights.shape[1]
    total = members * lax.axis_size("member")
    all_points = points * lax.axis_size("point")
    rows = round_up(fields, 8)
    span = members * LANES
    sent_rows = members * fields
    weights, truth = weights.T, truth.T
    shift, coef, area = shift[None], coef[None], area[None]
    tile = lambda shape: pl.BlockSpec((1,) + shape, lambda i: (i, 0, 0))
    shape = jax.ShapeDtypeStruct
    vmem = pl.BlockSpec(memory_space=pltpu.VMEM)
    hbm = pl.BlockSpec(memory_space=pltpu.HBM)
    core_swap = [(0, 1), (1, 0), (2, 3), (3, 2)]
    chip_swap = [(0, 2), (1, 3), (2, 0), (3, 1)]

    def forecast(n, first, us):
        return pl.pallas_call(
            functools.partial(forecast_kernel, first=first),
            in_specs=[hbm, hbm],
            out_specs=[vmem] * 3,
            out_shape=[
                shape((n, members, LANES, width), BF16),
                shape((n, rows, span), F32),
                shape((n, sent_rows, LANES), BF16),
            ],
            scratch_shapes=[
                pltpu.VMEM((fields, width), BF16),
                pltpu.SemaphoreType.DMA((n,)),
                pltpu.SemaphoreType.DMA,
            ],
            compiler_params=params(),
            cost_estimate=cost(us),
            name="forecast",
        )(hidden, pltpu.with_memory_space_constraint(weights, pltpu.HBM))

    def near(n, first, us, own, sib):
        return pl.pallas_call(
            functools.partial(near_kernel, first=first, members=members, total=total),
            in_specs=[vmem] * 6,
            out_specs=[vmem] * (2 if first else 3),
            out_shape=[shape((n, rows, span), F32), shape((8, LANES), F32)]
            + ([] if first else [shape((rows, LANES), F32)]),
            scratch_shapes=([pltpu.VMEM((rows, LANES), F32)] if first else [])
            + [pltpu.VMEM((n, rows, LANES), F32), pltpu.VMEM((1, LANES), F32)],
            compiler_params=params(),
            cost_estimate=cost(us),
            name="near",
        )(own, sib, truth, area, shift, coef)

    def direct(n, first, us, coefs, own, away, acc, loss):
        return pl.pallas_call(
            functools.partial(direct_kernel, first=first, members=members, total=total, fields=fields),
            in_specs=[vmem] * 6,
            out_specs=[vmem] * 2,
            out_shape=[shape((n, rows, span), F32), shape((8, LANES), F32)],
            compiler_params=params(),
            cost_estimate=cost(us),
            name="direct",
        )(own, away, acc, loss, area, coefs)

    def far(n, first, us, coefs, own, acc, loss, x, *sums, received, last=False):
        sums_shapes = [((rows, LANES), F32), ((8, LANES), F32)]
        if last:
            outs = [shape((width, LANES), BF16)]
            extra = [pltpu.VMEM(*i) for i in sums_shapes] + [pltpu.VMEM((LANES, LANES), F32)]
        else:
            outs = [shape((LANES, width), F32)] + [shape(*i) for i in sums_shapes]
            extra = []
        return pl.pallas_call(
            functools.partial(
                far_kernel, first=first, before=len(sums), received=len(received), last=last, members=members, total=total, fields=fields
            ),
            in_specs=[vmem] * (6 + len(sums) + len(received)),
            out_specs=[vmem] * (1 + len(outs)),
            out_shape=[shape((n, LANES, span), BF16)] + outs,
            scratch_shapes=[pltpu.VMEM((n, LANES, span), F32)] + extra,
            compiler_params=params(),
            cost_estimate=cost(us),
            name="far",
        )(own, acc, area, coefs, loss, x, *sums, *received)

    across = lambda a: lax.ppermute(a, "member", chip_swap)
    beside = lambda a: lax.ppermute(a, "member", core_swap)
    hold = lax.optimization_barrier
    n0, n1, n2 = TILES
    a1, a2 = n0, n0 + n1
    x0, own0, out0 = forecast(n0, 0, US[0])
    away0 = across(out0)
    x1, own1, out1 = forecast(n1, a1, US[1])
    away1 = across(out1)
    x2, own2, out2 = forecast(n2, a2, US[2])
    own0, out2 = hold((own0, out2))
    away2 = across(out2)
    sib0, sib1, sib2 = beside(out0), beside(out1), beside(out2)
    acc0, loss0, coefs = near(n0, 0, US[3], own0, sib0)
    away0, acc0, own1, own2 = hold((away0, acc0, own1, own2))
    fwd0 = beside(away0)
    acc1, loss1 = near(n1, a1, US[4], own1, sib1)
    acc2, loss2 = near(n2, a2, US[7], own2, sib2)
    away1, acc1, acc0, acc2 = hold((away1, acc1, acc0, acc2))
    fwd1 = beside(away1)
    grad0, *sums = far(n0, 0, US[5], coefs, own0, acc0, loss0, x0, received=(away0, fwd0))
    grad1, *sums = far(n1, a1, US[6], coefs, own1, acc1, loss1, x1, *sums, received=(away1, fwd1))
    away2, acc2, *sums = hold((away2, acc2, *sums))
    fwd2 = beside(away2)
    acc2, loss2 = direct(n2, a2, US[9], coefs, own2, away2, acc2, loss2)
    grad2, packed = far(n2, a2, US[8], coefs, own2, acc2, loss2, x2, *sums, received=(fwd2,), last=True)
    grads = [grad0, grad1, grad2]

    parts = lax.all_to_all(packed, ("member", "point"), split_axis=0, concat_axis=0, tiled=True)

    grad = grads[0] if len(grads) == 1 else jnp.concatenate(grads, axis=0)
    slope = pl.pallas_call(
        slope_kernel,
        grid=(points // LANES,),
        in_specs=[tile((LANES, span)), pl.BlockSpec((fields, width), lambda i: (0, 0))],
        out_specs=pl.BlockSpec((members, LANES, width), lambda i: (0, i, 0)),
        out_shape=shape(hidden.shape, BF16),
        compiler_params=params(),
        cost_estimate=cost(5),
        name="slope",
    )(grad, weights)

    own_rows = width // (lax.axis_size("member") * lax.axis_size("point"))
    dw, bias, loss = pl.pallas_call(
        functools.partial(
            finish_kernel, fields=fields, scale=float((total * all_points) ** -0.5), count=float(all_points * fields)
        ),
        out_shape=[shape((own_rows, fields), F32), shape((1, fields), F32), shape((1, 1), F32)],
        compiler_params=params(),
        name="finish",
    )(parts)
    return loss.reshape(()), slope, dw, bias.reshape(fields)


def solution(mesh):
    placed = (P("member", "point", None), P(), P(), P("point", None), P("point"), P())
    return jax.shard_map(
        shards,
        mesh=mesh,
        in_specs=placed,
        out_specs=(P(), P("member", "point", None), P(("member", "point"), None), P()),
        check_vma=False,
    )
```

```python
import functools

import jax
import jax.numpy as jnp
from jax import lax
from jax.experimental import pallas as pl
from jax.experimental.pallas import tpu as pltpu
from jax.sharding import PartitionSpec as P

F32 = jnp.float32
BF16 = jnp.bfloat16
LANES = 128
TILES = (2, 2, 2)
US = (.01,.01,.01,.01,8,8,.01,.01,.01,8)
SMOOTH = 0.05 * 0.05
ALPHA = 0.95


def params(mib=48):
    return pltpu.CompilerParams(vmem_limit_bytes=mib * 1024 * 1024)


def round_up(n, k):
    return -(-n // k) * k


def add_length(spread, b, m, n, members, folded):
    turn = (m - n) % members
    if folded or turn in (0, members // 2):
        return spread + b
    return spread + 2.0 * b if turn < members // 2 else spread


def half_turn(a):
    return pltpu.roll(a, 4, 0)


def interleaved(f, members, fields):
    parts = lambda g: [f[8 * g : 8 * g + 8, m * LANES : (m + 1) * LANES] for m in range(members)]
    groups = [p for g in range(fields // 8) for p in parts(g)]
    ends = parts(fields // 8)
    groups += [ends[m] + half_turn(ends[m + 1]) for m in range(0, members, 2)]
    return jnp.concatenate(groups, axis=0).astype(BF16)


def others(ref, t, g, members, fields):
    count = members if 8 * g + 8 <= fields else members // 2
    block = ref[t, 8 * members * g : 8 * members * g + 8 * count, :].astype(F32)
    return [block[8 * n : 8 * n + 8] for n in range(count)]


def forecast_kernel(x_hbm, w_hbm, x, own_ref, sent_ref, w, x_sems, w_sem, *, first):
    tiles, members, _, width = x.shape
    rows = own_ref.shape[1]
    fields = w.shape[0]
    w_copy = pltpu.make_async_copy(w_hbm, w, w_sem)
    w_copy.start()

    def fetch(t):
        points = pl.ds((first + t) * LANES, LANES)
        return pltpu.make_async_copy(x_hbm.at[:, points], x.at[t], x_sems.at[t])

    for t in range(tiles):
        fetch(t).start()
    w_copy.wait()

    def step(t, carry):
        fetch(t).wait()
        f = lax.dot_general(
            x[t].reshape(members * LANES, width),
            w[...],
            (((1,), (1,)), ((), ())),
            preferred_element_type=F32,
        )
        f = jnp.concatenate([f, jnp.zeros((members * LANES, LANES - fields), F32)], axis=1)
        f = f.T[:rows]
        own_ref[t] = f
        sent_ref[t] = interleaved(f, members, fields)
        return carry

    lax.fori_loop(0, tiles, step, 0)


def column(row, rows):
    return jnp.broadcast_to(row, (LANES, LANES)).T[:rows]


def pad_row(ref, scratch, fields):
    scratch[...] = jnp.zeros_like(scratch)
    scratch[:, :fields] = ref[...]
    return scratch[...]


def slope_and_length(d):
    t = d * d + SMOOTH
    r = lax.rsqrt(t)
    return d * r, t * r


def near_kernel(own_ref, sib_ref, truth_ref, area_ref, shift_ref, coef_ref, acc_ref, loss_ref, coefs, goal, rpad, *, first, members, total):
    tiles, rows, _ = own_ref.shape
    fields = truth_ref.shape[0]
    c1 = (1.0 - (1.0 - ALPHA) / total) / (total - 1)
    c2 = (1.0 - (1.0 - ALPHA) / total) / (2.0 * total * (total - 1))

    here = slice(first * LANES, (first + tiles) * LANES)
    coefs[...] = column(pad_row(coef_ref, rpad, fields), rows)
    shifts = column(pad_row(shift_ref, rpad, fields), rows)
    goal[...] = jnp.zeros_like(goal)
    for t in range(tiles):
        at = slice((first + t) * LANES, (first + t + 1) * LANES)
        goal[t, :fields, :] = truth_ref[:, at] - shifts[:fields]
    loss_ref[...] = jnp.zeros_like(loss_ref)

    def step(t, carry):
        loss = jnp.zeros((8, LANES), F32)
        for g in range(rows // 8):
            span = slice(8 * g, 8 * g + 8)
            own = [own_ref[t, span, m * LANES : (m + 1) * LANES] for m in range(members)]
            sib = others(sib_ref, t, g, members, fields)
            folded = len(sib) < members
            skill = jnp.zeros((8, LANES), F32)
            spread = jnp.zeros((8, LANES), F32)
            inner = jnp.zeros((8, LANES), F32)
            slopes = [jnp.zeros((8, LANES), F32) for _ in range(members)]
            for m in range(members):
                mine = own[m] + half_turn(own[m]) if folded else own[m]
                for n, other in enumerate(sib):
                    a, b = slope_and_length(mine - other)
                    slopes[m] = slopes[m] + a
                    spread = add_length(spread, b, m, n, members, folded)
                if folded:
                    slopes[m] = slopes[m] + half_turn(slopes[m])
            if folded:
                spread = spread + half_turn(spread)
            for m in range(members):
                for n in range(m + 1, members):
                    a, b = slope_and_length(own[m] - own[n])
                    slopes[m] = slopes[m] + a
                    slopes[n] = slopes[n] - a
                    inner = inner + b
            for m in range(members):
                a, b = slope_and_length(own[m] - goal[t, span, :])
                skill = skill + b
                acc_ref[t, span, m * LANES : (m + 1) * LANES] = a - c1 * slopes[m]
            loss = loss + coefs[span] * (skill * (1.0 / total) - c2 * (spread + 2.0 * inner))
        at = pl.multiple_of((first + t) * LANES, LANES)
        loss_ref[...] += loss * area_ref[:, pl.ds(at, LANES)]
        return carry

    lax.fori_loop(0, tiles, step, 0)


def direct_kernel(own_ref, far_ref, acc_ref, loss_in, area_ref, coefs, out_ref, loss_ref, *, first, members, total, fields):
    tiles, rows, _ = own_ref.shape
    c1 = (1.0 - (1.0 - ALPHA) / total) / (total - 1)
    c2 = (1.0 - (1.0 - ALPHA) / total) / (2.0 * total * (total - 1))
    loss_ref[...] = loss_in[...]

    def step(t, carry):
        loss = jnp.zeros((8, LANES), F32)
        for g in range(rows // 8):
            span = slice(8 * g, 8 * g + 8)
            own = [own_ref[t, span, m * LANES : (m + 1) * LANES] for m in range(members)]
            remote = others(far_ref, t, g, members, fields)
            folded = len(remote) < members
            spread = jnp.zeros((8, LANES), F32)
            for m in range(members):
                mine = own[m] + half_turn(own[m]) if folded else own[m]
                slopes = jnp.zeros((8, LANES), F32)
                for n, other in enumerate(remote):
                    a, b = slope_and_length(mine - other)
                    slopes = slopes + a
                    spread = add_length(spread, b, m, n, members, folded)
                if folded:
                    slopes = slopes + half_turn(slopes)
                here = slice(m * LANES, (m + 1) * LANES)
                out_ref[t, span, here] = acc_ref[t, span, here] - c1 * slopes
            if folded:
                spread = spread + half_turn(spread)
            loss = loss + coefs[span] * spread
        at = pl.multiple_of((first + t) * LANES, LANES)
        loss_ref[...] -= c2 * loss * area_ref[:, pl.ds(at, LANES)]
        return carry

    lax.fori_loop(0, tiles, step, 0)


def pack(dw, bias_ref, loss_ref, padded, fields):
    padded[...] = jnp.zeros_like(padded)
    padded[: bias_ref.shape[0], :] = bias_ref[...]
    bias = jnp.sum(padded[...].T, axis=0, keepdims=True)
    loss = jnp.sum(jnp.sum(loss_ref[...], axis=0, keepdims=True), axis=1, keepdims=True)
    high = loss.astype(BF16).astype(F32)
    low = loss - high
    quarter = fields // 4
    lane = lax.broadcasted_iota(jnp.int32, (8, LANES), 1)
    row = lax.broadcasted_iota(jnp.int32, (8, LANES), 0) % 4
    bias = jnp.broadcast_to(bias, (8, LANES))
    extra = jnp.zeros((8, LANES), F32)
    for r in range(4):
        moved = pltpu.roll(bias, fields - quarter * r, 1)
        extra = jnp.where(row == r, moved, extra)
    extra = jnp.where(lane < fields + quarter, extra, 0.0)
    at = lane == fields + quarter
    extra = jnp.where(at & (row == 0), high, extra)
    extra = jnp.where(at & (row == 1), low, extra)
    table = dw.T.reshape(-1, 8, LANES)
    keep = lax.broadcasted_iota(jnp.int32, table.shape, 2) < fields
    table = jnp.where(keep, table, extra[None])
    return table.reshape(-1, LANES).astype(BF16)


def far_kernel(*refs, first, before, received, last, members, total, fields):
    own_ref, acc_ref, area_ref, coefs, near_loss, x = refs[:6]
    earlier, refs = refs[6 : 6 + before], refs[6 + before :]
    sources, refs = refs[:received], refs[received:]
    if last:
        grad_ref, out_ref, grads, bias_ref, loss_ref, padded = refs
    else:
        grad_ref, dw_ref, bias_ref, loss_ref, grads = refs
    tiles, rows, _ = own_ref.shape
    width = x.shape[3]
    span_all = members * LANES
    c1 = (1.0 - (1.0 - ALPHA) / total) / (total - 1)
    c2 = (1.0 - (1.0 - ALPHA) / total) / (2.0 * total * (total - 1))

    grads[:, rows:, :] = jnp.zeros((tiles, LANES - rows, span_all), F32)
    if before:
        bias_ref[...] = earlier[1][...]
        loss_ref[...] = earlier[2][...] + near_loss[...]
    else:
        bias_ref[...] = jnp.zeros_like(bias_ref)
        loss_ref[...] = near_loss[...]

    def step(t, carry):
        at = pl.multiple_of((first + t) * LANES, LANES)
        area = jnp.broadcast_to(area_ref[:, pl.ds(at, LANES)], (8, LANES))
        loss = jnp.zeros((8, LANES), F32)
        for g in range(rows // 8):
            span = slice(8 * g, 8 * g + 8)
            own = [own_ref[t, span, m * LANES : (m + 1) * LANES] for m in range(members)]
            remote = [o for ref in sources for o in others(ref, t, g, members, fields)]
            folded = len(remote) < received * members
            spread = jnp.zeros((8, LANES), F32)
            scale = coefs[span] * area
            bias = jnp.zeros((8, LANES), F32)
            for m in range(members):
                mine = own[m] + half_turn(own[m]) if folded else own[m]
                slopes = jnp.zeros((8, LANES), F32)
                for n, other in enumerate(remote):
                    a, b = slope_and_length(mine - other)
                    slopes = slopes + a
                    spread = add_length(spread, b, m, n, members, folded)
                if folded:
                    slopes = slopes + half_turn(slopes)
                here = slice(m * LANES, (m + 1) * LANES)
                grad = (scale * (acc_ref[t, span, here] - c1 * slopes)).astype(BF16).astype(F32)
                grads[t, span, here] = grad
                bias = bias + grad
            if folded:
                spread = spread + half_turn(spread)
            bias_ref[span, :] += bias
            loss = loss + coefs[span] * spread
        loss_ref[...] -= c2 * loss * area
        grad_ref[t] = grads[t].astype(BF16)
        return carry

    lax.fori_loop(0, tiles, step, 0)

    dw = earlier[0][...] if before else jnp.zeros((LANES, width), F32)
    for t in range(tiles):
        dw = dw + jnp.dot(grad_ref[t], x[t].reshape(span_all, width), preferred_element_type=F32)
    if last:
        out_ref[...] = pack(dw, bias_ref, loss_ref, padded, fields)
    else:
        dw_ref[...] = dw


def slope_kernel(grad_ref, w_ref, out_ref):
    fields = w_ref.shape[0]
    s = lax.dot_general(
        grad_ref[0, :fields, :], w_ref[...], (((0,), (0,)), ((), ())), preferred_element_type=F32
    )
    out_ref[...] = s.astype(BF16).reshape(out_ref.shape)


def finish_kernel(parts_ref, dw_ref, bias_ref, loss_ref, *, fields, scale, count):
    parts = parts_ref[...].astype(F32).reshape(-1, 8, LANES)
    total = jnp.sum(parts, axis=0)
    total = total[:4] + total[4:]
    dw_ref[...] = total[:, :fields] * scale
    quarter = fields // 4
    lane = lax.broadcasted_iota(jnp.int32, (1, LANES), 1)
    bias = jnp.zeros((1, LANES), F32)
    for r in range(4):
        moved = pltpu.roll(total, (quarter * r - fields) % LANES, 1)[r : r + 1]
        bias = jnp.where((lane >= quarter * r) & (lane < quarter * (r + 1)), moved, bias)
    bias_ref[...] = bias[:, :fields] * scale
    at = fields + quarter
    loss_ref[...] = (total[0:1, at : at + 1] + total[1:2, at : at + 1]) * (1.0 / count)


def cost(us):
    return pl.CostEstimate(flops=int(us * 1e9), bytes_accessed=int(us * 3.5e6), transcendentals=0)


def shards(hidden, weights, shift, truth, area, coef):
    members, points, width = hidden.shape
    fields = weights.shape[1]
    total = members * lax.axis_size("member")
    all_points = points * lax.axis_size("point")
    rows = round_up(fields, 8)
    span = members * LANES
    sent_rows = members * fields
    weights, truth = weights.T, truth.T
    shift, coef, area = shift[None], coef[None], area[None]
    tile = lambda shape: pl.BlockSpec((1,) + shape, lambda i: (i, 0, 0))
    shape = jax.ShapeDtypeStruct
    vmem = pl.BlockSpec(memory_space=pltpu.VMEM)
    hbm = pl.BlockSpec(memory_space=pltpu.HBM)
    core_swap = [(0, 1), (1, 0), (2, 3), (3, 2)]
    chip_swap = [(0, 2), (1, 3), (2, 0), (3, 1)]

    def forecast(n, first, us):
        return pl.pallas_call(
            functools.partial(forecast_kernel, first=first),
            in_specs=[hbm, hbm],
            out_specs=[vmem] * 3,
            out_shape=[
                shape((n, members, LANES, width), BF16),
                shape((n, rows, span), F32),
                shape((n, sent_rows, LANES), BF16),
            ],
            scratch_shapes=[
                pltpu.VMEM((fields, width), BF16),
                pltpu.SemaphoreType.DMA((n,)),
                pltpu.SemaphoreType.DMA,
            ],
            compiler_params=params(),
            cost_estimate=cost(us),
            name="forecast",
        )(hidden, pltpu.with_memory_space_constraint(weights, pltpu.HBM))

    def near(n, first, us, own, sib):
        return pl.pallas_call(
            functools.partial(near_kernel, first=first, members=members, total=total),
            in_specs=[vmem] * 6,
            out_specs=[vmem] * (2 if first else 3),
            out_shape=[shape((n, rows, span), F32), shape((8, LANES), F32)]
            + ([] if first else [shape((rows, LANES), F32)]),
            scratch_shapes=([pltpu.VMEM((rows, LANES), F32)] if first else [])
            + [pltpu.VMEM((n, rows, LANES), F32), pltpu.VMEM((1, LANES), F32)],
            compiler_params=params(),
            cost_estimate=cost(us),
            name="near",
        )(own, sib, truth, area, shift, coef)

    def direct(n, first, us, coefs, own, away, acc, loss):
        return pl.pallas_call(
            functools.partial(direct_kernel, first=first, members=members, total=total, fields=fields),
            in_specs=[vmem] * 6,
            out_specs=[vmem] * 2,
            out_shape=[shape((n, rows, span), F32), shape((8, LANES), F32)],
            compiler_params=params(),
            cost_estimate=cost(us),
            name="direct",
        )(own, away, acc, loss, area, coefs)

    def far(n, first, us, coefs, own, acc, loss, x, *sums, received, last=False):
        sums_shapes = [((rows, LANES), F32), ((8, LANES), F32)]
        if last:
            outs = [shape((width, LANES), BF16)]
            extra = [pltpu.VMEM(*i) for i in sums_shapes] + [pltpu.VMEM((LANES, LANES), F32)]
        else:
            outs = [shape((LANES, width), F32)] + [shape(*i) for i in sums_shapes]
            extra = []
        return pl.pallas_call(
            functools.partial(
                far_kernel, first=first, before=len(sums), received=len(received), last=last, members=members, total=total, fields=fields
            ),
            in_specs=[vmem] * (6 + len(sums) + len(received)),
            out_specs=[vmem] * (1 + len(outs)),
            out_shape=[shape((n, LANES, span), BF16)] + outs,
            scratch_shapes=[pltpu.VMEM((n, LANES, span), F32)] + extra,
            compiler_params=params(),
            cost_estimate=cost(us),
            name="far",
        )(own, acc, area, coefs, loss, x, *sums, *received)

    across = lambda a: lax.ppermute(a, "member", chip_swap)
    beside = lambda a: lax.ppermute(a, "member", core_swap)
    hold = lax.optimization_barrier
    n0, n1, n2 = TILES
    a1, a2 = n0, n0 + n1
    x0, own0, out0 = forecast(n0, 0, US[0])
    away0 = across(out0)
    x1, own1, out1 = forecast(n1, a1, US[1])
    away1 = across(out1)
    x2, own2, out2 = forecast(n2, a2, US[2])
    own0, out2 = hold((own0, out2))
    away2 = across(out2)
    sib0, sib1, sib2 = beside(out0), beside(out1), beside(out2)
    acc0, loss0, coefs = near(n0, 0, US[3], own0, sib0)
    away0, acc0, own1, own2 = hold((away0, acc0, own1, own2))
    fwd0 = beside(away0)
    acc1, loss1 = near(n1, a1, US[4], own1, sib1)
    acc2, loss2 = near(n2, a2, US[7], own2, sib2)
    away1, acc1, acc0, acc2 = hold((away1, acc1, acc0, acc2))
    fwd1 = beside(away1)
    grad0, *sums = far(n0, 0, US[5], coefs, own0, acc0, loss0, x0, received=(away0, fwd0))
    grad1, *sums = far(n1, a1, US[6], coefs, own1, acc1, loss1, x1, *sums, received=(away1, fwd1))
    away2, acc2, *sums = hold((away2, acc2, *sums))
    fwd2 = beside(away2)
    acc2, loss2 = direct(n2, a2, US[9], coefs, own2, away2, acc2, loss2)
    grad2, packed = far(n2, a2, US[8], coefs, own2, acc2, loss2, x2, *sums, received=(fwd2,), last=True)
    grads = [grad0, grad1, grad2]

    parts = lax.all_to_all(packed, ("member", "point"), split_axis=0, concat_axis=0, tiled=True)

    grad = grads[0] if len(grads) == 1 else jnp.concatenate(grads, axis=0)
    slope = pl.pallas_call(
        slope_kernel,
        grid=(points // LANES,),
        in_specs=[tile((LANES, span)), pl.BlockSpec((fields, width), lambda i: (0, 0))],
        out_specs=pl.BlockSpec((members, LANES, width), lambda i: (0, i, 0)),
        out_shape=shape(hidden.shape, BF16),
        compiler_params=params(),
        cost_estimate=cost(5),
        name="slope",
    )(grad, weights)

    own_rows = width // (lax.axis_size("member") * lax.axis_size("point"))
    dw, bias, loss = pl.pallas_call(
        functools.partial(
            finish_kernel, fields=fields, scale=float((total * all_points) ** -0.5), count=float(all_points * fields)
        ),
        out_shape=[shape((own_rows, fields), F32), shape((1, fields), F32), shape((1, 1), F32)],
        compiler_params=params(),
        name="finish",
    )(parts)
    return loss.reshape(()), slope, dw, bias.reshape(fields)


def solution(mesh):
    placed = (P("member", "point", None), P(), P(), P("point", None), P("point"), P())
    return jax.shard_map(
        shards,
        mesh=mesh,
        in_specs=placed,
        out_specs=(P(), P("member", "point", None), P(("member", "point"), None), P()),
        check_vma=False,
    )
```
